256 devices in a mesh: frame: 8 (over z_hi, y), space: 32 (over z_lo, x, core).
Axes of the slice: x: 4, y: 4, z: 8 (z_hi: 2, z_lo: 4; z = z_hi * 4 + z_lo), core: 2. Of those that a mesh axis runs over, the one named last changes fastest.
Arguments:
- query: bfloat16 [32, 32, 4, 8, 1536], P('frame', 'space'), may hold values from -6 to 6
- key: bfloat16 [32, 32, 4, 8, 1536], P('frame', 'space'), may hold values from -6 to 6
- value: bfloat16 [32, 32, 4, 8, 1536], P('frame', 'space'), may hold values from -6 to 6
- grad_out: bfloat16 [32, 32, 4, 8, 1536], P('frame', 'space'), may hold values from -1.5 to 1.5
- log_norm: float32 [32, 32, 4, 8, 12], P('frame', 'space'), may hold values from 3 to 5
- delta: float32 [32, 32, 4, 8, 12], P('frame', 'space'), may hold values from -12 to 12
- tile_valid: int32 [16], replicated, may hold values from 1 to 4
Outputs:
- grad_query: bfloat16 [32, 32, 4, 8, 1536], P('frame', 'space')
- grad_key: bfloat16 [32, 32, 4, 8, 1536], P('frame', 'space')
- grad_value: bfloat16 [32, 32, 4, 8, 1536], P('frame', 'space')
The draws below stay inside these ranges and needn't reach their ends.
All inputs are finite; a program needn't handle non-finite values.
Results may differ from the reference program's by a relative error of at most 0.0049.
Values may be sent and summed in bfloat16 or wider, within the bound.
No kernel may reach another device: no remote copies, remote signals or barrier semaphores. Data moves between devices by JAX's collectives and lax.ppermute only.
A program may use at most 192 MiB of HBM per device.

```python
import math
import jax
import jax.numpy as jnp
from jax import lax

HEADS = 12
HEAD_DIM = 128
TILE = 4
SPACE_W = 4
WIDTH = 1536
BCOLS = 8
ROW_BLOCKS = 8
SPACE_BLOCKS = 32
FRAMES = 32
ROWS = 32
COLS = 32
FRAME_TILES = 8
ROW_TILES = 8


def place_ends(drawn, key, low, high):
    place = [jax.random.randint(jax.random.fold_in(key, axis), (), 0, length) for axis, length in enumerate(drawn.shape)]
    longest = drawn.shape.index(max(drawn.shape))
    beside = place[:longest] + [(place[longest] + 1) % drawn.shape[longest]] + place[longest + 1:]
    return drawn.at[tuple(place)].set(low).at[tuple(beside)].set(high)


def block_levels(key, shape, split, low, top_value):
    def one(position, blocks):
        steps = jax.random.uniform(jax.random.fold_in(jax.random.fold_in(key, 6), position), (blocks,), jnp.float32, low / len(split), top_value / len(split))
        return jnp.repeat(jnp.exp(steps), shape[position] // blocks).reshape((-1,) + (1,) * (len(shape) - position - 1))

    factor_of = one(*split[0])
    for cut in split[1:]:
        factor_of = factor_of * one(*cut)
    return factor_of


def scatter_about(key, dims, scale, limit, split=(), kind=jnp.bfloat16):
    entries = jax.random.normal(key, dims, jnp.float32) * scale
    if len(split) > 0:
        entries = block_levels(key, dims, split, -0.22, 0.18) * entries
    return jnp.clip(entries, min=-limit, max=limit).astype(kind)


def setup_inputs(seed: int = 0) -> dict:
    streams_of = jax.random.split(jax.random.key(seed), 8)
    query = scatter_about(streams_of[0], (FRAMES, SPACE_BLOCKS, TILE, BCOLS, WIDTH), 1.0, 6.0, ((0, 8), (1, 32)))
    key = scatter_about(streams_of[1], (FRAMES, SPACE_BLOCKS, TILE, BCOLS, WIDTH), 1.0, 6.0, ((0, 8), (1, 32)))
    value = scatter_about(streams_of[2], (FRAMES, SPACE_BLOCKS, TILE, BCOLS, WIDTH), 1.0, 6.0, ((0, 8), (1, 32)))
    grad_out = scatter_about(streams_of[3], (FRAMES, SPACE_BLOCKS, TILE, BCOLS, WIDTH), 0.25, 1.5, ((0, 8), (1, 32)))
    log_norm = jnp.clip(3.0 + 2.0 * jax.random.uniform(streams_of[4], (FRAMES, SPACE_BLOCKS, TILE, BCOLS, HEADS), jnp.float32) ** block_levels(streams_of[4], (FRAMES, SPACE_BLOCKS, TILE, BCOLS, HEADS), ((0, 8), (1, 32)), -0.2, 0.2), 3.0, 5.0)
    delta = scatter_about(streams_of[5], (FRAMES, SPACE_BLOCKS, TILE, BCOLS, HEADS), 2.0, 12.0, ((0, 8), (1, 32)), jnp.float32)
    tile_valid = place_ends(jax.random.randint(streams_of[6], (FRAME_TILES + ROW_TILES,), 1, 5), jax.random.fold_in(streams_of[6], 1), 1, 4).astype(jnp.int32)
    return {"query": query, "key": key, "value": value, "grad_out": grad_out, "log_norm": log_norm, "delta": delta, "tile_valid": tile_valid}


def to_grid(blocks):
    frames = blocks.shape[0]
    last = blocks.shape[-1]
    grid = blocks.reshape(frames, ROW_BLOCKS, SPACE_W, TILE, BCOLS, last)
    grid = grid.transpose(0, 1, 3, 2, 4, 5)
    return grid.reshape(frames, ROWS, COLS, last)

def to_blocks(grid):
    last = grid.shape[-1]
    blocks = grid.reshape(FRAMES, ROW_BLOCKS, TILE, SPACE_W, BCOLS, last)
    blocks = blocks.transpose(0, 1, 3, 2, 4, 5)
    return blocks.reshape(FRAMES, SPACE_BLOCKS, TILE, BCOLS, last)

def valid_line(table, extent):
    where_at = jnp.arange(extent, dtype=jnp.int32)
    return where_at % TILE < jnp.repeat(table, TILE)

def split_heads(rows):
    return rows.reshape(rows.shape[0], HEADS, HEAD_DIM).astype(jnp.float32)

def widen_half(values):
    narrow = lax.optimization_barrier(values.astype(jnp.bfloat16))
    return narrow.astype(jnp.float32)

def flatten_heads(values):
    return values.reshape(values.shape[0], HEADS * HEAD_DIM).astype(jnp.bfloat16)

def tile_grads(own, near, own_mask, near_mask):
    scaling = 1.0 / math.sqrt(HEAD_DIM)
    own_query, own_key, own_value, own_out = [split_heads(part) for part in own[:4]]
    own_norm, own_delta = (own[4], own[5])
    near_query, near_key, near_value, near_out = [split_heads(part) for part in near[:4]]
    near_norm, near_delta = (near[4], near[5])
    pair_mask = own_mask[:, None] & near_mask[None, :]
    scores = jnp.einsum('qhd,khd->hqk', own_query, near_key) * scaling
    probs = jnp.where(pair_mask[None], jnp.exp(scores - own_norm.T[:, :, None]), 0.0)
    grad_probs = jnp.einsum('qhd,khd->hqk', own_out, near_value)
    grad_scores = widen_half(probs * (grad_probs - own_delta.T[:, :, None]))
    grad_query = jnp.einsum('hqk,khd->qhd', grad_scores, near_key) * scaling
    back_mask = near_mask[:, None] & own_mask[None, :]
    back_scores = jnp.einsum('qhd,khd->hqk', near_query, own_key) * scaling
    back_probs = jnp.where(back_mask[None], jnp.exp(back_scores - near_norm.T[:, :, None]), 0.0)
    probs_half = widen_half(back_probs)
    grad_value = jnp.einsum('hqk,qhd->khd', probs_half, near_out)
    back_grad = jnp.einsum('qhd,khd->hqk', near_out, own_value)
    back_slope = widen_half(back_probs * (back_grad - near_delta.T[:, :, None]))
    grad_key = jnp.einsum('hqk,qhd->khd', back_slope, near_query) * scaling
    return (flatten_heads(grad_query), flatten_heads(grad_key), flatten_heads(grad_value))

def reference(query, key, value, grad_out, log_norm, delta, tile_valid):
    frame_valid = tile_valid[:FRAME_TILES]
    row_valid = tile_valid[FRAME_TILES:]
    padding = ((TILE, TILE), (TILE, TILE), (TILE, TILE), (0, 0))
    grids = [jnp.pad(to_grid(part), padding) for part in (query, key, value, grad_out, log_norm, delta)]
    frame_ok = valid_line(frame_valid, FRAMES)
    row_ok = valid_line(row_valid, ROWS)
    usable = frame_ok[:, None, None] & row_ok[None, :, None] & jnp.ones((1, 1, COLS), dtype=bool)
    usable = jnp.pad(usable, TILE)
    row_tiles = ROWS // TILE
    col_tiles = COLS // TILE
    tile_count = FRAMES // TILE * row_tiles * col_tiles

    def one_tile(tile_index):
        frame_tile = tile_index // (row_tiles * col_tiles)
        row_tile = tile_index // col_tiles % row_tiles
        col_tile = tile_index % col_tiles

        def cut(part, offset, extent):
            starts = [frame_tile * TILE + offset, row_tile * TILE + offset, col_tile * TILE + offset]
            sizes = [extent, extent, extent]
            if part.ndim == 4:
                starts = starts + [jnp.zeros((), jnp.int32)]
                sizes = sizes + [part.shape[3]]
                return lax.dynamic_slice(part, starts, sizes).reshape(extent ** 3, part.shape[3])
            return lax.dynamic_slice(part, starts, sizes).reshape(extent ** 3)
        own = [cut(part, TILE, TILE) for part in grids]
        near = [cut(part, 0, 3 * TILE) for part in grids]
        return tile_grads(own, near, cut(usable, TILE, TILE), cut(usable, 0, 3 * TILE))
    tiles = lax.map(one_tile, jnp.arange(tile_count, dtype=jnp.int32))

    def assemble(pieces):
        grid = pieces.reshape(FRAMES // TILE, row_tiles, col_tiles, TILE, TILE, TILE, HEADS * HEAD_DIM)
        grid = grid.transpose(0, 3, 1, 4, 2, 5, 6).reshape(FRAMES, ROWS, COLS, HEADS * HEAD_DIM)
        return to_blocks(grid)
    return (assemble(tiles[0]), assemble(tiles[1]), assemble(tiles[2]))
```

```python
import functools
import math

import jax
import jax.numpy as jnp
from jax import lax
from jax.experimental import pallas as pl
from jax.experimental.pallas import tpu as pltpu
from jax.sharding import PartitionSpec as P

HEAD_DIM = 128
GROUPS = 4
GROUP_HEADS = 3
COL_BLOCKS = 4
TOKENS = 128
HALF = 64
STAT_ROWS = 16
SCALE = 1.0 / math.sqrt(HEAD_DIM)
LOG2E = math.log2(math.e)
GROUP_WIDTH = GROUP_HEADS * HEAD_DIM
VMEM_LIMIT = 56 * 1024 * 1024

SMEM_SPEC = pl.BlockSpec(memory_space=pltpu.SMEM)


def reorder_matrix(frame_valid, row_valid):
    tiled = lax.broadcasted_iota(jnp.int32, (TOKENS, TOKENS), 0)
    stored = lax.broadcasted_iota(jnp.int32, (TOKENS, TOKENS), 1)
    tile, frame = tiled >> 6, (tiled >> 4) & 3
    row, col = (tiled >> 2) & 3, tiled & 3
    same = stored == frame * 32 + row * 8 + tile * 4 + col
    keep = same & (frame < frame_valid) & (row < row_valid)
    return jnp.where(keep, 1.0, 0.0)


def reorder_back(frame_valid, row_valid):
    stored = lax.broadcasted_iota(jnp.int32, (TOKENS, TOKENS), 0)
    tiled = lax.broadcasted_iota(jnp.int32, (TOKENS, TOKENS), 1)
    tile, frame = tiled >> 6, (tiled >> 4) & 3
    row, col = (tiled >> 2) & 3, tiled & 3
    same = stored == frame * 32 + row * 8 + tile * 4 + col
    keep = same & (frame < frame_valid) & (row < row_valid)
    return jnp.where(keep, 1.0, 0.0)


def group_lanes(group):
    return pl.ds(pl.multiple_of(group * GROUP_WIDTH, HEAD_DIM), GROUP_WIDTH)


def pack_pair(place, first, second, outs, matrix):
    for m in range(GROUPS):
        lanes = group_lanes(place ^ m)
        for part, ref in enumerate((first, second)):
            moved = jnp.dot(matrix, ref[:, lanes], preferred_element_type=jnp.float32)
            moved = moved.astype(jnp.bfloat16)
            for h in range(GROUP_HEADS):
                outs[m][h, part * TOKENS : (part + 1) * TOKENS, :] = moved[
                    :, h * HEAD_DIM : (h + 1) * HEAD_DIM
                ]


def pack_plain_kernel(where, first, second, *outs):
    matrix = reorder_matrix(where[1], where[2]).astype(jnp.bfloat16)
    pack_pair(where[0], first, second, outs, matrix)


def pack_stat_kernel(where, first, second, log_norm, delta, *rest):
    outs, table = rest[:GROUPS], rest[GROUPS]
    matrix = reorder_matrix(where[1], where[2]).astype(jnp.bfloat16)
    pack_pair(where[0], first, second, outs, matrix)
    table[...] = jnp.zeros_like(table)
    for base, stat in ((0, log_norm[...] * LOG2E), (3, delta[...])):
        left = stat
        for step in range(3):
            piece = left.astype(jnp.bfloat16)
            left = left - piece.astype(jnp.float32)
            moved = jnp.dot(matrix, piece, preferred_element_type=jnp.float32)
            turned = moved.T
            for head in range(GROUPS * GROUP_HEADS):
                table[head, base + step : base + step + 1, :] = turned[head : head + 1, :]
    for m in range(GROUPS):
        group = where[0] ^ m
        for h in range(GROUP_HEADS):
            outs[m][h, 2 * TOKENS :, :] = table[group * GROUP_HEADS + h].astype(jnp.bfloat16)


def vmem_specs(count):
    return [pl.BlockSpec(memory_space=pltpu.VMEM)] * count


def pack_plain(where, first, second):
    shape = jax.ShapeDtypeStruct((GROUP_HEADS, 2 * TOKENS, HEAD_DIM), jnp.bfloat16)
    return pl.pallas_call(
        pack_plain_kernel,
        out_shape=[shape] * GROUPS,
        in_specs=[SMEM_SPEC] + vmem_specs(2),
        out_specs=vmem_specs(GROUPS),
        compiler_params=pltpu.CompilerParams(vmem_limit_bytes=VMEM_LIMIT),
        name="pack_kv",
    )(where, first, second)


def pack_stat(where, first, second, log_norm, delta):
    shape = jax.ShapeDtypeStruct((GROUP_HEADS, 2 * TOKENS + STAT_ROWS, HEAD_DIM), jnp.bfloat16)
    return pl.pallas_call(
        pack_stat_kernel,
        out_shape=[shape] * GROUPS,
        in_specs=[SMEM_SPEC] + vmem_specs(4),
        out_specs=vmem_specs(GROUPS),
        scratch_shapes=[pltpu.VMEM((GROUPS * GROUP_HEADS, STAT_ROWS, TOKENS), jnp.float32)],
        compiler_params=pltpu.CompilerParams(vmem_limit_bytes=VMEM_LIMIT),
        name="pack_qd",
    )(where, first, second, log_norm, delta)


def dot_t(a, b):
    return lax.dot_general(a, b, (((1,), (1,)), ((), ())), preferred_element_type=jnp.float32)


def dot(a, b):
    return jnp.dot(a, b, preferred_element_type=jnp.float32)


def window(column):
    pieces = []
    if column > 0:
        pieces.append((column - 1, HALF, TOKENS))
    pieces.append((column, 0, TOKENS))
    if column < COL_BLOCKS - 1:
        pieces.append((column + 1, 0, HALF))
    return pieces


def near_rows(cell, slots, column, offset):
    parts = [cell[slots[b], 0, offset + lo : offset + hi, :] for b, lo, hi in window(column)]
    return jnp.concatenate(parts, axis=0)


def near_stat(cell, slots, column, base):
    parts = []
    for b, lo, hi in window(column):
        rows = cell[slots[b], 0, 2 * TOKENS :, :].astype(jnp.float32)
        total = rows[base : base + 1] + rows[base + 1 : base + 2] + rows[base + 2 : base + 3]
        parts.append(total[:, lo:hi])
    return jnp.concatenate(parts, axis=1)


def tile_mask(column):
    extent = sum(hi - lo for _, lo, hi in window(column))
    skip = 1 if column > 0 else 0
    own = lax.broadcasted_iota(jnp.int32, (TOKENS, extent), 0) >> 6
    near = (lax.broadcasted_iota(jnp.int32, (TOKENS, extent), 1) >> 6) - skip
    return (own - near <= 1) & (near - own <= 1)


def query_kernel(where, own, *rest):
    cells, out = rest[:-1], rest[-1]
    slots = [where[3] ^ b for b in range(COL_BLOCKS)]
    for column in range(COL_BLOCKS):
        slot = slots[column]
        query = own[slot, 0, :TOKENS, :]
        grad = own[slot, 0, TOKENS : 2 * TOKENS, :]
        stat = own[slot, 0, 2 * TOKENS :, :].astype(jnp.float32).T
        norm = stat[:, 0:1] + stat[:, 1:2] + stat[:, 2:3]
        delta = stat[:, 3:4] + stat[:, 4:5] + stat[:, 5:6]
        mask = tile_mask(column)
        total = jnp.zeros((TOKENS, HEAD_DIM), jnp.float32)
        for cell in cells:
            keys = near_rows(cell, slots, column, 0)
            values = near_rows(cell, slots, column, TOKENS)
            probs = jnp.exp2(dot_t(query, keys) * (SCALE * LOG2E) - norm)
            probs = jnp.where(mask, probs, 0.0)
            slope = probs * (dot_t(grad, values) - delta)
            total = total + dot(slope.astype(jnp.bfloat16), keys)
        out[slot, 0] = (total * SCALE).astype(jnp.bfloat16)


def key_kernel(where, own, *rest):
    cells, out = rest[:-1], rest[-1]
    slots = [where[3] ^ b for b in range(COL_BLOCKS)]
    for column in range(COL_BLOCKS):
        slot = slots[column]
        key = own[slot, 0, :TOKENS, :]
        value = own[slot, 0, TOKENS : 2 * TOKENS, :]
        mask = tile_mask(column)
        key_total = jnp.zeros((TOKENS, HEAD_DIM), jnp.float32)
        value_total = jnp.zeros((TOKENS, HEAD_DIM), jnp.float32)
        for cell in cells:
            queries = near_rows(cell, slots, column, 0)
            grads = near_rows(cell, slots, column, TOKENS)
            norm = near_stat(cell, slots, column, 0)
            delta = near_stat(cell, slots, column, 3)
            probs = jnp.exp2(dot_t(key, queries) * (SCALE * LOG2E) - norm)
            probs = jnp.where(mask, probs, 0.0)
            value_total = value_total + dot(probs.astype(jnp.bfloat16), grads)
            slope = probs * (dot_t(value, grads) - delta)
            key_total = key_total + dot(slope.astype(jnp.bfloat16), queries)
        out[slot, 0, :TOKENS, :] = (key_total * SCALE).astype(jnp.bfloat16)
        out[slot, 0, TOKENS:, :] = value_total.astype(jnp.bfloat16)


def attend(kernel, name, where, own, cells, out_rows, flops):
    def spec(array):
        rows = array.shape[2]
        return pl.BlockSpec((COL_BLOCKS, 1, rows, HEAD_DIM), lambda h: (0, h, 0, 0))

    return pl.pallas_call(
        kernel,
        grid=(GROUP_HEADS,),
        out_shape=jax.ShapeDtypeStruct(
            (COL_BLOCKS, GROUP_HEADS, out_rows, HEAD_DIM), jnp.bfloat16
        ),
        in_specs=[SMEM_SPEC, spec(own)] + [spec(cell) for cell in cells],
        out_specs=pl.BlockSpec((COL_BLOCKS, 1, out_rows, HEAD_DIM), lambda h: (0, h, 0, 0)),
        compiler_params=pltpu.CompilerParams(vmem_limit_bytes=VMEM_LIMIT),
        cost_estimate=pl.CostEstimate(flops=flops, bytes_accessed=8 << 20, transcendentals=0),
        name=name,
    )(where, own, *cells)


def unpack_kernel(parts, where, *rest):
    messages, outs = rest[:GROUPS], rest[GROUPS:]
    matrix = reorder_back(where[1], where[2]).astype(jnp.bfloat16)
    for m in range(GROUPS):
        lanes = group_lanes(where[0] ^ m)
        for part in range(parts):
            block = jnp.concatenate(
                [
                    messages[m][h, part * TOKENS : (part + 1) * TOKENS, :]
                    for h in range(GROUP_HEADS)
                ],
                axis=1,
            )
            outs[part][:, lanes] = dot(matrix, block).astype(jnp.bfloat16)


def unpack(name, where, messages, parts):
    shape = jax.ShapeDtypeStruct((TOKENS, GROUPS * GROUP_WIDTH), jnp.bfloat16)
    return pl.pallas_call(
        functools.partial(unpack_kernel, parts),
        out_shape=[shape] * parts,
        in_specs=[SMEM_SPEC] + vmem_specs(GROUPS),
        out_specs=vmem_specs(parts),
        compiler_params=pltpu.CompilerParams(vmem_limit_bytes=VMEM_LIMIT),
        name=name,
    )(where, *messages)


def exchange_route(m, space_count):
    route = []
    for s in range(space_count):
        z, high, column = s // 8, (s // 4) % 2, s % 4
        route.append((s, z * 8 + (column ^ m) * 2 + high))
    return route


def core_route(space_count):
    return [(s, s ^ 1) for s in range(space_count)]


def row_route(space_count):
    route = []
    for s in range(1, space_count - 8, 2):
        route += [(s, s + 7), (s + 7, s)]
    return route


def frame_route(frame_count, step):
    return [(f, f + step) for f in range(frame_count) if 0 <= f + step < frame_count]


def spread(messages):
    count = lax.axis_size("space")
    arrived = [lax.ppermute(v, "space", exchange_route(m, count)) for m, v in enumerate(messages)]
    return jnp.stack(arrived)


def gather_back(array):
    count = lax.axis_size("space")
    back = [[(b, a) for a, b in exchange_route(m, count)] for m in range(GROUPS)]
    return [lax.ppermute(array[m], "space", back[m]) for m in range(GROUPS)]


def cells_of(own):
    frames, spaces = lax.axis_size("frame"), lax.axis_size("space")
    column = [own] + [
        lax.ppermute(own, "frame", frame_route(frames, step)) for step in (1, -1)
    ]
    cells = []
    for cell in column:
        cells += [
            cell,
            lax.ppermute(cell, "space", core_route(spaces)),
            lax.ppermute(cell, "space", row_route(spaces)),
        ]
    return cells


def shards(query, key, value, grad_out, log_norm, delta, tile_valid):
    frame_at = lax.axis_index("frame")
    space_at = lax.axis_index("space")
    frame_count = lax.axis_size("frame")
    shape = query.shape
    where = jnp.stack(
        [
            space_at % 4,
            tile_valid[frame_at],
            tile_valid[frame_count + space_at // 4],
            (space_at // 2) % 4,
        ]
    ).astype(jnp.int32)

    def flat(array):
        return array.reshape(TOKENS, array.shape[-1])

    own_kv = spread(pack_plain(where, flat(key), flat(value)))
    own_qd = spread(
        pack_stat(where, flat(query), flat(grad_out), flat(log_norm), flat(delta))
    )
    kv_cells = cells_of(own_kv)
    qd_cells = cells_of(own_qd)
    unit = 2 * 64 * 1728 * 128 * 8 * 3
    grad_q = attend(query_kernel, "query_side", where, own_qd, kv_cells, TOKENS, 3 * unit)
    grad_kv = attend(key_kernel, "key_side", where, own_kv, qd_cells, 2 * TOKENS, 4 * unit)
    (out_q,) = unpack("unpack_q", where, gather_back(grad_q), 1)
    out_k, out_v = unpack("unpack_kv", where, gather_back(grad_kv), 2)
    return (out_q.reshape(shape), out_k.reshape(shape), out_v.reshape(shape))


def solution(mesh):
    blocks = P("frame", "space", None, None, None)
    return jax.shard_map(
        shards,
        mesh=mesh,
        in_specs=(blocks,) * 6 + (P(),),
        out_specs=(blocks,) * 3,
        check_vma=False,
    )
```

```python
import functools
import math

import jax
import jax.numpy as jnp
from jax import lax
from jax.experimental import pallas as pl
from jax.experimental.pallas import tpu as pltpu
from jax.sharding import PartitionSpec as P

HEADS = 12
HEAD_DIM = 128
CHIPS = 16
BLOCKS = 4
FRAMES = 4
TOKENS = 128
HALF = 64
STAT_ROWS = 16
KV_ROWS = 2 * TOKENS
QD_ROWS = 2 * TOKENS + STAT_ROWS
SCALE = 1.0 / math.sqrt(HEAD_DIM)
LOG2E = math.log2(math.e)
VMEM_LIMIT = 56 * 1024 * 1024
AXES = ("frame", "space")

SMEM_SPEC = pl.BlockSpec(memory_space=pltpu.SMEM)


def vmem_specs(count):
    return [pl.BlockSpec(memory_space=pltpu.VMEM)] * count


def params():
    return pltpu.CompilerParams(vmem_limit_bytes=VMEM_LIMIT)


def keep_matrix(tile_valid, stored_dim):
    frame_valid = tile_valid[lax.axis_index("frame")]
    row_valid = tile_valid[lax.axis_size("frame") + lax.axis_index("space") // 4]
    tiled = lax.broadcasted_iota(jnp.int32, (TOKENS, TOKENS), 1 - stored_dim)
    stored = lax.broadcasted_iota(jnp.int32, (TOKENS, TOKENS), stored_dim)
    tile, frame = tiled >> 6, (tiled >> 4) & 3
    row, col = (tiled >> 2) & 3, tiled & 3
    same = stored == frame * 32 + row * 8 + tile * 4 + col
    keep = same & (frame < frame_valid) & (row < row_valid)
    return jnp.where(keep, 1.0, 0.0).astype(jnp.bfloat16)


def dot_t(a, b):
    return lax.dot_general(a, b, (((1,), (1,)), ((), ())), preferred_element_type=jnp.float32)


def dot(a, b):
    return jnp.dot(a, b, preferred_element_type=jnp.float32)


def pack_pair(matrix, first, second, out):
    for part, ref in enumerate((first, second)):
        moved = dot(matrix, ref[...]).astype(jnp.bfloat16)
        for head in range(HEADS):
            out[head, part * TOKENS : (part + 1) * TOKENS, :] = moved[
                :, head * HEAD_DIM : (head + 1) * HEAD_DIM
            ]
    out[HEADS:] = jnp.zeros((CHIPS - HEADS,) + out.shape[1:], jnp.bfloat16)


def pack_kv_kernel(tile_valid, first, second, out):
    pack_pair(keep_matrix(tile_valid, 1), first, second, out)


def pack_qd_kernel(tile_valid, first, second, log_norm, delta, out, table):
    matrix = keep_matrix(tile_valid, 1)
    pack_pair(matrix, first, second, out)
    table[...] = jnp.zeros_like(table)
    for base, stat in ((0, log_norm[...] * LOG2E), (3, delta[...])):
        left = stat
        for step in range(3):
            piece = left.astype(jnp.bfloat16)
            left = left - piece.astype(jnp.float32)
            turned = dot(matrix, piece).T
            for head in range(HEADS):
                table[head, base + step : base + step + 1, :] = turned[head : head + 1, :]
    out[:HEADS, 2 * TOKENS :, :] = table[...].astype(jnp.bfloat16)


def pack_kv(tile_valid, first, second):
    return pl.pallas_call(
        pack_kv_kernel,
        out_shape=jax.ShapeDtypeStruct((CHIPS, KV_ROWS, HEAD_DIM), jnp.bfloat16),
        in_specs=[SMEM_SPEC] + vmem_specs(2),
        out_specs=vmem_specs(1)[0],
        compiler_params=params(),
        name="pack_kv",
    )(tile_valid, first, second)


def pack_qd(tile_valid, first, second, log_norm, delta):
    return pl.pallas_call(
        pack_qd_kernel,
        out_shape=jax.ShapeDtypeStruct((CHIPS, QD_ROWS, HEAD_DIM), jnp.bfloat16),
        in_specs=[SMEM_SPEC] + vmem_specs(4),
        out_specs=vmem_specs(1)[0],
        scratch_shapes=[pltpu.VMEM((HEADS, STAT_ROWS, TOKENS), jnp.float32)],
        compiler_params=params(),
        name="pack_qd",
    )(tile_valid, first, second, log_norm, delta)


def window(column):
    pieces = []
    if column > 0:
        pieces.append((column - 1, HALF, TOKENS))
    pieces.append((column, 0, TOKENS))
    if column < BLOCKS - 1:
        pieces.append((column + 1, 0, HALF))
    return pieces


def near_rows(near, column, offset):
    parts = [near(b, offset + lo, offset + hi) for b, lo, hi in window(column)]
    return jnp.concatenate(parts, axis=0)


def near_stat(near, column, offset, base):
    parts = []
    for b, lo, hi in window(column):
        rows = near(b, offset, offset + STAT_ROWS).astype(jnp.float32)
        total = rows[base : base + 1] + rows[base + 1 : base + 2] + rows[base + 2 : base + 3]
        parts.append(total[:, lo:hi])
    return jnp.concatenate(parts, axis=1)


def tile_mask(column):
    extent = sum(hi - lo for _, lo, hi in window(column))
    skip = 1 if column > 0 else 0
    own = lax.broadcasted_iota(jnp.int32, (TOKENS, extent), 0) >> 6
    near = (lax.broadcasted_iota(jnp.int32, (TOKENS, extent), 1) >> 6) - skip
    return (own - near <= 1) & (near - own <= 1)


def reader(ref, *index):
    return lambda block, lo, hi: ref[(*index, block, slice(lo, hi), slice(None))]


def query_step(own, own_frame, nears, offset, totals):
    for column in range(BLOCKS):
        query = own[own_frame, column, :TOKENS, :]
        grad = own[own_frame, column, TOKENS : 2 * TOKENS, :]
        stat = own[own_frame, column, 2 * TOKENS :, :].astype(jnp.float32).T
        mask = tile_mask(column)
        norm = jnp.broadcast_to(stat[:, 0:1] + stat[:, 1:2] + stat[:, 2:3], mask.shape)
        delta = jnp.broadcast_to(stat[:, 3:4] + stat[:, 4:5] + stat[:, 5:6], mask.shape)
        total = totals[own_frame, column]
        for near in nears:
            keys = near_rows(near, column, offset)
            values = near_rows(near, column, offset + TOKENS)
            probs = jnp.exp2(dot_t(query, keys) * (SCALE * LOG2E) - norm)
            probs = jnp.where(mask, probs, 0.0)
            slope = probs * (dot_t(grad, values) - delta)
            total = total + dot(slope.astype(jnp.bfloat16), keys)
        totals[own_frame, column] = total


def key_step(own, own_frame, nears, offset, key_totals, value_totals):
    for column in range(BLOCKS):
        key = own[own_frame, column, :TOKENS, :]
        value = own[own_frame, column, TOKENS : 2 * TOKENS, :]
        mask = tile_mask(column)
        key_total = key_totals[own_frame, column]
        value_total = value_totals[own_frame, column]
        for near in nears:
            queries = near_rows(near, column, offset)
            grads = near_rows(near, column, offset + TOKENS)
            norm = near_stat(near, column, offset + 2 * TOKENS, 0)
            delta = near_stat(near, column, offset + 2 * TOKENS, 3)
            probs = jnp.exp2(dot_t(key, queries) * (SCALE * LOG2E) - norm)
            probs = jnp.where(mask, probs, 0.0)
            value_total = value_total + dot(probs.astype(jnp.bfloat16), grads)
            slope = probs * (dot_t(value, grads) - delta)
            key_total = key_total + dot(slope.astype(jnp.bfloat16), queries)
        key_totals[own_frame, column] = key_total
        value_totals[own_frame, column] = value_total


def frame_pairs(step):
    def body(t, carry):
        own_frame = (t + 1) // 3
        step(own_frame, t - 2 * own_frame)
        return carry

    lax.fori_loop(0, 3 * FRAMES - 2, body, 0)


def query_kernel(own, *rest):
    nears, totals = rest[:-1], rest[-1]
    totals[...] = jnp.zeros_like(totals)
    frame_pairs(
        lambda a, b: query_step(own, a, [reader(near, b) for near in nears], 0, totals)
    )


def key_kernel(own, *rest):
    nears, (key_totals, value_totals) = rest[:-2], rest[-2:]
    key_totals[...] = jnp.zeros_like(key_totals)
    value_totals[...] = jnp.zeros_like(value_totals)
    frame_pairs(
        lambda a, b: key_step(
            own, a, [reader(near, b) for near in nears], 0, key_totals, value_totals
        )
    )


def last_kernel(own_kv, own_qd, row_qd, jump_own, jump_core, jump_row, *rest):
    query_in, key_in, value_in, out, query_totals, key_totals, value_totals = rest
    query_totals[...] = query_in[...]
    key_totals[...] = key_in[...]
    value_totals[...] = value_in[...]
    frame_pairs(
        lambda a, b: key_step(own_kv, a, [reader(row_qd, b)], 0, key_totals, value_totals)
    )
    edge = jnp.where(lax.axis_index("frame") < FRAMES, FRAMES - 1, 0)
    jumped = [reader(jump_own), reader(jump_core), reader(jump_row)]
    query_step(own_qd, edge, jumped, 0, query_totals)
    key_step(own_kv, edge, jumped, KV_ROWS, key_totals, value_totals)
    for frame in range(FRAMES):
        for column in range(BLOCKS):
            high, core = column // 2, column % 2
            parts = (
                query_totals[frame, column] * SCALE,
                key_totals[frame, column] * SCALE,
                value_totals[frame, column],
            )
            for part, total in enumerate(parts):
                out[core, frame, high, part * TOKENS : (part + 1) * TOKENS, :] = total.astype(
                    jnp.bfloat16
                )


TOTALS = jax.ShapeDtypeStruct((FRAMES, BLOCKS, TOKENS, HEAD_DIM), jnp.float32)


def attend(kernel, name, args, out_shape, pairs, scratch=()):
    flops = pairs * 2 * TOKENS * HEAD_DIM * 256
    return pl.pallas_call(
        kernel,
        out_shape=out_shape,
        in_specs=vmem_specs(len(args)),
        out_specs=jax.tree.map(lambda _: vmem_specs(1)[0], out_shape),
        scratch_shapes=scratch,
        compiler_params=params(),
        cost_estimate=pl.CostEstimate(
            flops=flops * 8, bytes_accessed=6 << 20, transcendentals=pairs << 15
        ),
        name=name,
    )(*args)


def unpack_kernel(tile_valid, blocks, *outs):
    matrix = keep_matrix(tile_valid, 0)
    for part, out in enumerate(outs):
        rows = slice(part * TOKENS, (part + 1) * TOKENS)
        joined = jnp.concatenate([blocks[head, rows, :] for head in range(HEADS)], axis=1)
        out[...] = dot(matrix, joined).astype(jnp.bfloat16)


def unpack(tile_valid, blocks):
    shape = jax.ShapeDtypeStruct((TOKENS, HEADS * HEAD_DIM), jnp.bfloat16)
    return pl.pallas_call(
        unpack_kernel,
        out_shape=[shape] * 3,
        in_specs=[SMEM_SPEC] + vmem_specs(1),
        out_specs=vmem_specs(3),
        compiler_params=params(),
        name="unpack",
    )(tile_valid, blocks)


def plane_exchange(array):
    spaces = lax.axis_size("space")
    groups = []
    for half in range(lax.axis_size("frame") // FRAMES):
        for z in range(spaces // 8):
            for core in range(2):
                groups.append(
                    [
                        (half * FRAMES + j // 4) * spaces + z * 8 + (j % 4) * 2 + core
                        for j in range(CHIPS)
                    ]
                )
    return lax.all_to_all(array, AXES, 0, 0, axis_index_groups=groups)


def core_swap(array):
    return lax.ppermute(array, "space", [(s, s ^ 1) for s in range(lax.axis_size("space"))])


def row_swap(array):
    route = []
    for s in range(1, lax.axis_size("space") - 8, 2):
        if s % 2 == 1:
            route += [(s, s + 7), (s + 7, s)]
    return lax.ppermute(array, "space", route)


def half_swap(array):
    count = lax.axis_size("frame")
    return lax.ppermute(array, "frame", [(f, (f + FRAMES) % count) for f in range(count)])


def two_ways(core, mine, other, axis):
    first = jnp.where(core == 0, mine, other)
    second = jnp.where(core == 0, other, mine)
    return jnp.stack([first, second], axis=axis)


def spread(packed, core):
    arrived = plane_exchange(packed).reshape(FRAMES, 2, 2, *packed.shape[1:])
    mine = lax.dynamic_index_in_dim(arrived, core, 1, keepdims=False)
    other = lax.dynamic_index_in_dim(arrived, 1 - core, 1, keepdims=False)
    whole = two_ways(core, mine, core_swap(other), 2)
    return whole.reshape(FRAMES, BLOCKS, *packed.shape[1:])


def shards(query, key, value, grad_out, log_norm, delta, tile_valid):
    core = lax.axis_index("space") % 2
    edge = jnp.where(lax.axis_index("frame") < FRAMES, FRAMES - 1, 0)
    shape = query.shape

    def flat(array):
        return array.reshape(TOKENS, array.shape[-1])

    own_kv = spread(pack_kv(tile_valid, flat(key), flat(value)), core)
    own_qd = spread(
        pack_qd(tile_valid, flat(query), flat(grad_out), flat(log_norm), flat(delta)), core
    )
    row_kv = row_swap(own_kv)
    core_kv = core_swap(own_kv)
    border = jnp.concatenate(
        [
            lax.dynamic_index_in_dim(own_kv, edge, 0, keepdims=False),
            lax.dynamic_index_in_dim(own_qd, edge, 0, keepdims=False),
        ],
        axis=1,
    )
    jump_own = half_swap(border)
    core_qd = core_swap(own_qd)
    row_qd = row_swap(own_qd)
    jump_core = core_swap(jump_own)
    jump_row = row_swap(jump_own)

    query_part = attend(
        query_kernel, "query_side", (own_qd, own_kv, core_kv, row_kv), TOTALS, 360
    )
    key_part, value_part = attend(
        key_kernel, "key_side", (own_kv, own_qd, core_qd), [TOTALS] * 2, 320
    )
    grads = attend(
        last_kernel,
        "last_part",
        (own_kv, own_qd, row_qd, jump_own, jump_core, jump_row, query_part, key_part, value_part),
        jax.ShapeDtypeStruct((2, FRAMES, 2, 3 * TOKENS, HEAD_DIM), jnp.bfloat16),
        240,
        [pltpu.VMEM(TOTALS.shape, TOTALS.dtype)] * 3,
    )
    mine = lax.dynamic_index_in_dim(grads, core, 0, keepdims=False)
    other = lax.dynamic_index_in_dim(grads, 1 - core, 0, keepdims=False)
    whole = two_ways(core, mine, core_swap(other), 1)
    blocks = plane_exchange(whole.reshape(CHIPS, 3 * TOKENS, HEAD_DIM))
    return tuple(out.reshape(shape) for out in unpack(tile_valid, blocks))


def solution(mesh):
    blocks = P("frame", "space", None, None, None)
    return jax.shard_map(
        shards,
        mesh=mesh,
        in_specs=(blocks,) * 6 + (P(),),
        out_specs=(blocks,) * 3,
        check_vma=False,
    )
```

```python
import functools
import math

import jax
import jax.numpy as jnp
from jax import lax
from jax.experimental import pallas as pl
from jax.experimental.pallas import tpu as pltpu
from jax.sharding import PartitionSpec as P

HEADS = 12
HEAD_DIM = 128
CHIPS = 16
BLOCKS = 4
FRAMES = 4
TOKENS = 128
HALF = 64
STAT_ROWS = 16
KEY, VALUE, QUERY, GRAD, STAT = (part * TOKENS for part in range(5))
ROWS = STAT + STAT_ROWS
SCALE = 1.0 / math.sqrt(HEAD_DIM)
LOG2E = math.log2(math.e)
VMEM_LIMIT = 56 * 1024 * 1024
FILL_FLOPS = 1 << 34
AXES = ("frame", "space")

SMEM_SPEC = pl.BlockSpec(memory_space=pltpu.SMEM)


def vmem_specs(count):
    return [pl.BlockSpec(memory_space=pltpu.VMEM)] * count


def params():
    return pltpu.CompilerParams(vmem_limit_bytes=VMEM_LIMIT)


def keep_matrix(tile_valid, stored_dim):
    frame_valid = tile_valid[lax.axis_index("frame")]
    row_valid = tile_valid[lax.axis_size("frame") + lax.axis_index("space") // 4]
    tiled = lax.broadcasted_iota(jnp.int32, (TOKENS, TOKENS), 1 - stored_dim)
    stored = lax.broadcasted_iota(jnp.int32, (TOKENS, TOKENS), stored_dim)
    tile, frame = tiled >> 6, (tiled >> 4) & 3
    row, col = (tiled >> 2) & 3, tiled & 3
    same = stored == frame * 32 + row * 8 + tile * 4 + col
    keep = same & (frame < frame_valid) & (row < row_valid)
    return jnp.where(keep, 1.0, 0.0).astype(jnp.bfloat16)


def dot_t(a, b):
    return lax.dot_general(a, b, (((1,), (1,)), ((), ())), preferred_element_type=jnp.float32)


def dot(a, b):
    return jnp.dot(a, b, preferred_element_type=jnp.float32)


def pack_part(matrix, start, ref, out):
    moved = dot(matrix, ref[...]).astype(jnp.bfloat16)
    for head in range(HEADS):
        out[head, start : start + TOKENS, :] = moved[:, head * HEAD_DIM : (head + 1) * HEAD_DIM]


def fill(heads, out):
    out[:HEADS] = heads[...]
    out[HEADS:] = jnp.zeros((CHIPS - HEADS,) + out.shape[1:], jnp.bfloat16)


def pack_kernel(tile_valid, key, value, query, grad, log_norm, delta, out, filled, table):
    matrix = keep_matrix(tile_valid, 1)
    for start, ref in ((KEY, key), (VALUE, value), (QUERY, query), (GRAD, grad)):
        pack_part(matrix, start, ref, out)
    table[...] = jnp.zeros_like(table)
    for base, stat in ((0, log_norm[...] * LOG2E), (3, delta[...])):
        left = stat
        for step in range(3):
            piece = left.astype(jnp.bfloat16)
            left = left - piece.astype(jnp.float32)
            turned = dot(matrix, piece).T
            for head in range(HEADS):
                table[head, base + step : base + step + 1, :] = turned[head : head + 1, :]
    out[:, STAT:, :] = table[...].astype(jnp.bfloat16)
    fill(out, filled)


HEADS_SHAPE = jax.ShapeDtypeStruct((HEADS, ROWS, HEAD_DIM), jnp.bfloat16)
FILLED_SHAPE = jax.ShapeDtypeStruct((CHIPS, ROWS, HEAD_DIM), jnp.bfloat16)


def pack(tile_valid, *arrays):
    return pl.pallas_call(
        pack_kernel,
        out_shape=[HEADS_SHAPE, FILLED_SHAPE],
        in_specs=[SMEM_SPEC] + vmem_specs(len(arrays)),
        out_specs=vmem_specs(2),
        scratch_shapes=[pltpu.VMEM((HEADS, STAT_ROWS, TOKENS), jnp.float32)],
        compiler_params=params(),
        name="pack",
    )(tile_valid, *arrays)


def refill(heads):
    return pl.pallas_call(
        fill,
        out_shape=FILLED_SHAPE,
        in_specs=vmem_specs(1),
        out_specs=vmem_specs(1)[0],
        compiler_params=params(),
        cost_estimate=pl.CostEstimate(
            flops=FILL_FLOPS, bytes_accessed=FILL_FLOPS >> 8, transcendentals=0
        ),
        name="refill",
    )(heads)


def window(column):
    pieces = []
    if column > 0:
        pieces.append((column - 1, HALF, TOKENS))
    pieces.append((column, 0, TOKENS))
    if column < BLOCKS - 1:
        pieces.append((column + 1, 0, HALF))
    return pieces


def near_rows(near, column, offset):
    parts = [near(b, offset + lo, offset + hi) for b, lo, hi in window(column)]
    return jnp.concatenate(parts, axis=0)


def near_stat(near, column, base):
    parts = []
    for b, lo, hi in window(column):
        rows = near(b, STAT, ROWS).astype(jnp.float32)
        total = rows[base : base + 1] + rows[base + 1 : base + 2] + rows[base + 2 : base + 3]
        parts.append(total[:, lo:hi])
    return jnp.concatenate(parts, axis=1)


def tile_mask(column):
    extent = sum(hi - lo for _, lo, hi in window(column))
    skip = 1 if column > 0 else 0
    own = lax.broadcasted_iota(jnp.int32, (TOKENS, extent), 0) >> 6
    near = (lax.broadcasted_iota(jnp.int32, (TOKENS, extent), 1) >> 6) - skip
    return (own - near <= 1) & (near - own <= 1)


def reader(ref, *index):
    return lambda block, lo, hi: ref[(*index, block, slice(lo, hi), slice(None))]


def near_all(nears, column, offset):
    return jnp.concatenate([near_rows(near, column, offset) for near in nears], axis=0)


def near_all_stat(nears, column, base):
    return jnp.concatenate([near_stat(near, column, base) for near in nears], axis=1)


def tile_masks(column, own_count, near_count):
    one = jnp.where(tile_mask(column), 1.0, 0.0)
    line = jnp.concatenate([one] * near_count, axis=1)
    return jnp.concatenate([line] * own_count, axis=0) > 0.5


def query_sum(own, nears, column):
    query = own(column, QUERY, QUERY + TOKENS)
    grad = own(column, GRAD, GRAD + TOKENS)
    stat = own(column, STAT, ROWS).astype(jnp.float32).T
    norm = stat[:, 0:1] + stat[:, 1:2] + stat[:, 2:3]
    delta = stat[:, 3:4] + stat[:, 4:5] + stat[:, 5:6]
    keys = near_all(nears, column, KEY)
    values = near_all(nears, column, VALUE)
    probs = jnp.exp2(dot_t(query, keys) * (SCALE * LOG2E) - norm)
    probs = jnp.where(tile_masks(column, 1, len(nears)), probs, 0.0)
    slope = probs * (dot_t(grad, values) - delta)
    return dot(slope.astype(jnp.bfloat16), keys)


def key_sum(owns, nears, column):
    key = jnp.concatenate([own(column, KEY, KEY + TOKENS) for own in owns], axis=0)
    value = jnp.concatenate([own(column, VALUE, VALUE + TOKENS) for own in owns], axis=0)
    queries = near_all(nears, column, QUERY)
    grads = near_all(nears, column, GRAD)
    norm = near_all_stat(nears, column, 0)
    delta = near_all_stat(nears, column, 3)
    probs = jnp.exp2(dot_t(key, queries) * (SCALE * LOG2E) - norm)
    probs = jnp.where(tile_masks(column, len(owns), len(nears)), probs, 0.0)
    value_sum = dot(probs.astype(jnp.bfloat16), grads)
    slope = probs * (dot_t(value, grads) - delta)
    return dot(slope.astype(jnp.bfloat16), queries), value_sum


def add_key_sums(totals, frames, column, parts):
    for i, frame in enumerate(frames):
        for total, part in zip(totals, parts):
            total[frame, column] += part[i * TOKENS : (i + 1) * TOKENS]


def by_core(ref, *index):
    return lambda block, lo, hi: ref[(block % 2, *index, block // 2, slice(lo, hi))]


def by_column(ref, *index):
    return lambda block, lo, hi: ref[(*index, block // 2, block % 2, slice(lo, hi))]


def frames_near(frame):
    return [f for f in range(FRAMES) if abs(f - frame) <= 1]


def edge_frame():
    return jnp.where(lax.axis_index("frame") < FRAMES, FRAMES - 1, 0)


def place(scratch, core, arrived, swapped):
    scratch[core] = arrived
    scratch[1 - core] = swapped


def first_query_kernel(arrived, swapped, total, blocks):
    core = lax.axis_index("space") % 2
    place(blocks, core, arrived[...], swapped[...])
    for frame in range(FRAMES):
        nears = [by_core(blocks, f, row) for f in frames_near(frame) for row in range(2)]
        for column in range(BLOCKS):
            total[frame, column] = query_sum(by_core(blocks, frame, core), nears, column)


def first_key_kernel(arrived, swapped, key_total, value_total, blocks):
    core = lax.axis_index("space") % 2
    place(blocks, core, arrived[...], swapped[...])
    key_total[...] = jnp.zeros_like(key_total)
    value_total[...] = jnp.zeros_like(value_total)
    for column in range(BLOCKS):
        for f in range(FRAMES):
            frames = frames_near(f)
            owns = [by_core(blocks, frame, core) for frame in frames]
            parts = key_sum(owns, [by_core(blocks, f, 0), by_core(blocks, f, 1)], column)
            add_key_sums((key_total, value_total), frames, column, parts)


def last_kernel(arrived, swapped, row, row_swapped, jump, jump_swapped, jump_row, *rest):
    firsts, (mine, other), rest = rest[:3], rest[3:5], rest[5:]
    own, near, jumped, jumped_row, done, first_totals, *totals, sems = rest
    core = lax.axis_index("space") % 2
    lower = lax.axis_index("frame") < FRAMES
    moves = [
        (arrived.at[:, core], own.at[core]),
        (swapped.at[:, core], own.at[1 - core]),
        (row.at[:, 1 - core], near.at[core]),
        (row_swapped, near.at[1 - core]),
        (jump, jumped.at[core]),
        (jump_swapped, jumped.at[1 - core]),
        (jump_row, jumped_row),
    ] + [(first, first_totals.at[i]) for i, first in enumerate(firsts)]
    copies = [pltpu.make_async_copy(*move, sems.at[i]) for i, move in enumerate(moves)]
    for copy in copies:
        copy.start()
    for total in totals[1:]:
        total[...] = jnp.zeros_like(total)
    for copy in copies[:4]:
        copy.wait()
    for column in range(BLOCKS):
        for f in range(FRAMES):
            frames = frames_near(f)
            owns = [by_core(own, frame) for frame in frames]
            parts = key_sum(owns, [by_core(near, f)], column)
            add_key_sums(totals[1:], frames, column, parts)
    for copy in copies[4:7]:
        copy.wait()
    frames = [jnp.where(lower, FRAMES - 1 - d, d) for d in range(FRAMES)]
    jumps = [by_core(jumped, 0), by_core(jumped, 1), by_column(jumped_row)]
    for column in range(BLOCKS):
        parts = key_sum([by_core(own, frames[0])], jumps, column)
        add_key_sums(totals[1:], frames[:1], column, parts)
    for d in range(FRAMES):
        nears = [by_core(near, frames[e]) for e in frames_near(d)] + (jumps if d == 0 else [])
        for column in range(BLOCKS):
            totals[0][frames[d], column] = query_sum(by_core(own, frames[d]), nears, column)
    for copy in copies[7:]:
        copy.wait()
    for part, (total, scale) in enumerate(zip(totals, (SCALE, SCALE, 1.0))):
        rows = slice(part * TOKENS, (part + 1) * TOKENS)
        for column in range(BLOCKS):
            both = (total[:, column] + first_totals[part, :, column]) * scale
            done[column % 2, :, column // 2, rows, :] = both.astype(jnp.bfloat16)
    mine[...] = done[core]
    other[...] = done[1 - core]


KEY_FLOPS = 1 << 33
TOTALS = (FRAMES, BLOCKS, TOKENS, HEAD_DIM)
DONE = (FRAMES, 2, 3 * TOKENS, HEAD_DIM)


def attend(kernel, name, flops, args, in_specs, out_shape, scratch):
    return pl.pallas_call(
        kernel,
        out_shape=out_shape,
        in_specs=in_specs,
        out_specs=vmem_specs(len(out_shape)),
        scratch_shapes=scratch,
        compiler_params=params(),
        cost_estimate=pl.CostEstimate(flops=flops, bytes_accessed=flops >> 8, transcendentals=0),
        name=name,
    )(*args)


def first_part(kernel, name, parts, flops, *args):
    return attend(
        kernel,
        name,
        flops,
        args,
        vmem_specs(len(args)),
        [jax.ShapeDtypeStruct(TOTALS, jnp.float32)] * parts,
        [pltpu.VMEM((2, FRAMES, 2, 2, ROWS, HEAD_DIM), jnp.bfloat16)],
    )


def last_part(*args):
    return attend(
        last_kernel,
        "last_part",
        1 << 30,
        args,
        [pl.BlockSpec(memory_space=pl.ANY)] * len(args),
        [jax.ShapeDtypeStruct(DONE, jnp.bfloat16)] * 2,
        [
            pltpu.VMEM((2, FRAMES, 2, ROWS, HEAD_DIM), jnp.bfloat16),
            pltpu.VMEM((2, FRAMES, 2, ROWS, HEAD_DIM), jnp.bfloat16),
            pltpu.VMEM((2, 2, 2, ROWS, HEAD_DIM), jnp.bfloat16),
            pltpu.VMEM((2, 2, ROWS, HEAD_DIM), jnp.bfloat16),
            pltpu.VMEM((2, *DONE), jnp.bfloat16),
            pltpu.VMEM((3, *TOTALS), jnp.float32),
        ]
        + [pltpu.VMEM(TOTALS, jnp.float32)] * 3
        + [pltpu.SemaphoreType.DMA((len(args),))],
    )


def unpack_kernel(tile_valid, blocks, *outs):
    matrix = keep_matrix(tile_valid, 0)
    for part, out in enumerate(outs):
        rows = slice(part * TOKENS, (part + 1) * TOKENS)
        joined = jnp.concatenate([blocks[head, rows, :] for head in range(HEADS)], axis=1)
        out[...] = dot(matrix, joined).astype(jnp.bfloat16)


def unpack(tile_valid, blocks):
    shape = jax.ShapeDtypeStruct((TOKENS, HEADS * HEAD_DIM), jnp.bfloat16)
    return pl.pallas_call(
        unpack_kernel,
        out_shape=[shape] * 3,
        in_specs=[SMEM_SPEC] + vmem_specs(1),
        out_specs=vmem_specs(3),
        compiler_params=params(),
        name="unpack",
    )(tile_valid, blocks)


def plane_exchange(array):
    spaces = lax.axis_size("space")
    groups = []
    for half in range(lax.axis_size("frame") // FRAMES):
        for z in range(spaces // 8):
            for core in range(2):
                groups.append(
                    [
                        (half * FRAMES + j // 4) * spaces + z * 8 + (j % 4) * 2 + core
                        for j in range(CHIPS)
                    ]
                )
    return lax.all_to_all(array, AXES, 0, 0, axis_index_groups=groups)


def with_idle(array):
    return jnp.pad(array, ((0, CHIPS - HEADS), (0, 0), (0, 0)))


def core_swap(array):
    return lax.ppermute(array, "space", [(s, s ^ 1) for s in range(lax.axis_size("space"))])


def row_swap(array):
    route = []
    for s in range(1, lax.axis_size("space") - 8, 2):
        route += [(s, s + 7), (s + 7, s)]
    return lax.ppermute(array, "space", route)


def row_shift(array):
    count = lax.axis_size("space")
    route = [(s, s + (8 if s // 4 % 2 else -8)) for s in range(count)]
    return lax.ppermute(array, "space", [(a, b) for a, b in route if 0 <= b < count])


def half_swap(array):
    count = lax.axis_size("frame")
    return lax.ppermute(array, "frame", [(f, (f + FRAMES) % count) for f in range(count)])


def two_ways(core, mine, other, axis):
    first = jnp.where(core == 0, mine, other)
    second = jnp.where(core == 0, other, mine)
    return jnp.stack([first, second], axis=axis)


def own_row(core, arrived, swapped, axis):
    mine = lax.dynamic_index_in_dim(arrived, core, axis, keepdims=False)
    other = lax.dynamic_index_in_dim(swapped, core, axis, keepdims=False)
    return two_ways(core, mine, other, axis + 1)


def shards(query, key, value, grad_out, log_norm, delta, tile_valid):
    core = lax.axis_index("space") % 2
    shape = query.shape

    def flat(array):
        return array.reshape(TOKENS, array.shape[-1])

    heads, packed = pack(
        tile_valid, *(flat(v) for v in (key, value, query, grad_out, log_norm, delta))
    )
    shifted = refill(row_shift(heads))
    arrived = plane_exchange(packed)
    arrived, shifted = lax.optimization_barrier((arrived, shifted))
    arrived = arrived.reshape(FRAMES, 2, 2, ROWS, HEAD_DIM)
    jump = half_swap(lax.dynamic_index_in_dim(arrived, edge_frame(), 0, keepdims=False))
    swapped = core_swap(arrived)
    row = plane_exchange(shifted).reshape(FRAMES, 2, 2, ROWS, HEAD_DIM)
    first_q = first_part(first_query_kernel, "first_query", 1, 1 << 10, arrived, swapped)
    jump, first_q = lax.optimization_barrier((jump, first_q))
    jump_swapped = core_swap(jump)
    key_args, jump_swapped = lax.optimization_barrier(((arrived, swapped), jump_swapped))
    first_kv = first_part(first_key_kernel, "first_key", 2, KEY_FLOPS, *key_args)
    jump_row = row_swap(own_row(core, jump, jump_swapped, 0))
    row, first_kv, jump_row = lax.optimization_barrier((row, first_kv, jump_row))
    row_swapped = core_swap(lax.dynamic_index_in_dim(row, core, 1, keepdims=False))
    firsts = (*first_q, *first_kv)
    mine, other = last_part(
        arrived, swapped, row, row_swapped, jump, jump_swapped, jump_row, *firsts
    )
    whole = two_ways(core, mine, core_swap(other), 1)
    blocks = plane_exchange(whole.reshape(CHIPS, *mine.shape[2:]))
    return tuple(out.reshape(shape) for out in unpack(tile_valid, blocks))


def solution(mesh):
    blocks = P("frame", "space", None, None, None)
    return jax.shard_map(
        shards,
        mesh=mesh,
        in_specs=(blocks,) * 6 + (P(),),
        out_specs=(blocks,) * 3,
        check_vma=False,
    )
```

```python
import functools
import math

import jax
import jax.numpy as jnp
from jax import lax
from jax.experimental import pallas as pl
from jax.experimental.pallas import tpu as pltpu
from jax.sharding import PartitionSpec as P

HEADS = 12
HEAD_DIM = 128
CHIPS = 16
BLOCKS = 4
FRAMES = 4
TOKENS = 128
HALF = 64
STAT_ROWS = 16
KEY, VALUE, QUERY, GRAD, STAT = (part * TOKENS for part in range(5))
ROWS = STAT + STAT_ROWS
SCALE = 1.0 / math.sqrt(HEAD_DIM)
LOG2E = math.log2(math.e)
VMEM_LIMIT = 56 * 1024 * 1024
FILL_FLOPS = 1 << 34
AXES = ("frame", "space")

SMEM_SPEC = pl.BlockSpec(memory_space=pltpu.SMEM)


def vmem_specs(count):
    return [pl.BlockSpec(memory_space=pltpu.VMEM)] * count


def params():
    return pltpu.CompilerParams(vmem_limit_bytes=VMEM_LIMIT)


def keep_matrix(tile_valid, stored_dim):
    frame_valid = tile_valid[lax.axis_index("frame")]
    row_valid = tile_valid[lax.axis_size("frame") + lax.axis_index("space") // 4]
    tiled = lax.broadcasted_iota(jnp.int32, (TOKENS, TOKENS), 1 - stored_dim)
    stored = lax.broadcasted_iota(jnp.int32, (TOKENS, TOKENS), stored_dim)
    tile, frame = tiled >> 6, (tiled >> 4) & 3
    row, col = (tiled >> 2) & 3, tiled & 3
    same = stored == frame * 32 + row * 8 + tile * 4 + col
    keep = same & (frame < frame_valid) & (row < row_valid)
    return jnp.where(keep, 1.0, 0.0).astype(jnp.bfloat16)


def dot_t(a, b):
    return lax.dot_general(a, b, (((1,), (1,)), ((), ())), preferred_element_type=jnp.float32)


def dot(a, b):
    return jnp.dot(a, b, preferred_element_type=jnp.float32)


def pack_part(matrix, start, ref, out):
    moved = dot(matrix, ref[...]).astype(jnp.bfloat16)
    for head in range(HEADS):
        out[head, start : start + TOKENS, :] = moved[:, head * HEAD_DIM : (head + 1) * HEAD_DIM]


def fill(heads, out):
    out[:HEADS] = heads[...]
    out[HEADS:] = jnp.zeros((CHIPS - HEADS,) + out.shape[1:], jnp.bfloat16)


def pack_kernel(tile_valid, key, value, query, grad, log_norm, delta, out, filled, table):
    matrix = keep_matrix(tile_valid, 1)
    for start, ref in ((KEY, key), (VALUE, value), (QUERY, query), (GRAD, grad)):
        pack_part(matrix, start, ref, out)
    table[...] = jnp.zeros_like(table)
    for base, stat in ((0, log_norm[...] * LOG2E), (3, delta[...])):
        left = stat
        for step in range(3):
            piece = left.astype(jnp.bfloat16)
            left = left - piece.astype(jnp.float32)
            turned = dot(matrix, piece).T
            for head in range(HEADS):
                table[head, base + step : base + step + 1, :] = turned[head : head + 1, :]
    out[:, STAT:, :] = table[...].astype(jnp.bfloat16)
    fill(out, filled)


HEADS_SHAPE = jax.ShapeDtypeStruct((HEADS, ROWS, HEAD_DIM), jnp.bfloat16)
FILLED_SHAPE = jax.ShapeDtypeStruct((CHIPS, ROWS, HEAD_DIM), jnp.bfloat16)


def pack(tile_valid, *arrays):
    return pl.pallas_call(
        pack_kernel,
        out_shape=[HEADS_SHAPE, FILLED_SHAPE],
        in_specs=[SMEM_SPEC] + vmem_specs(len(arrays)),
        out_specs=vmem_specs(2),
        scratch_shapes=[pltpu.VMEM((HEADS, STAT_ROWS, TOKENS), jnp.float32)],
        compiler_params=params(),
        name="pack",
    )(tile_valid, *arrays)


def refill_kernel(heads, out, scratch, sems):
    pieces = [pl.ds(i * 3, 3) for i in range(HEADS // 3)]
    ins = [
        pltpu.make_async_copy(heads.at[piece], scratch.at[piece], sems.at[i])
        for i, piece in enumerate(pieces)
    ]
    for copy in ins:
        copy.start()
    scratch[HEADS:] = jnp.zeros((CHIPS - HEADS,) + out.shape[1:], jnp.bfloat16)
    pieces.append(pl.ds(HEADS, CHIPS - HEADS))
    outs = [
        pltpu.make_async_copy(scratch.at[piece], out.at[piece], sems.at[len(ins) + i])
        for i, piece in enumerate(pieces)
    ]
    outs[-1].start()
    for copy_in, copy_out in zip(ins, outs):
        copy_in.wait()
        copy_out.start()
    for copy in outs:
        copy.wait()


def refill(heads):
    return pl.pallas_call(
        refill_kernel,
        out_shape=FILLED_SHAPE,
        in_specs=[pl.BlockSpec(memory_space=pl.ANY)],
        out_specs=pl.BlockSpec(memory_space=pl.ANY),
        scratch_shapes=[
            pltpu.VMEM(FILLED_SHAPE.shape, jnp.bfloat16),
            pltpu.SemaphoreType.DMA((2 * (HEADS // 3) + 1,)),
        ],
        compiler_params=params(),
        cost_estimate=pl.CostEstimate(
            flops=FILL_FLOPS, bytes_accessed=FILL_FLOPS >> 8, transcendentals=0
        ),
        name="refill",
    )(heads)


def window(column):
    pieces = []
    if column > 0:
        pieces.append((column - 1, HALF, TOKENS))
    pieces.append((column, 0, TOKENS))
    if column < BLOCKS - 1:
        pieces.append((column + 1, 0, HALF))
    return pieces


def near_rows(near, column, offset):
    parts = [near(b, offset + lo, offset + hi) for b, lo, hi in window(column)]
    return jnp.concatenate(parts, axis=0)


def near_stat(near, column, base):
    parts = []
    for b, lo, hi in window(column):
        rows = near(b, STAT, ROWS).astype(jnp.float32)
        total = rows[base : base + 1] + rows[base + 1 : base + 2] + rows[base + 2 : base + 3]
        parts.append(total[:, lo:hi])
    return jnp.concatenate(parts, axis=1)


def tile_mask(column):
    extent = sum(hi - lo for _, lo, hi in window(column))
    skip = 1 if column > 0 else 0
    own = lax.broadcasted_iota(jnp.int32, (TOKENS, extent), 0) >> 6
    near = (lax.broadcasted_iota(jnp.int32, (TOKENS, extent), 1) >> 6) - skip
    return (own - near <= 1) & (near - own <= 1)


def reader(ref, *index):
    return lambda block, lo, hi: ref[(*index, block, slice(lo, hi), slice(None))]


def near_all(nears, column, offset):
    return jnp.concatenate([near_rows(near, column, offset) for near in nears], axis=0)


def near_all_stat(nears, column, base):
    return jnp.concatenate([near_stat(near, column, base) for near in nears], axis=1)


def tile_masks(column, own_count, near_count):
    one = jnp.where(tile_mask(column), 1.0, 0.0)
    line = jnp.concatenate([one] * near_count, axis=1)
    return jnp.concatenate([line] * own_count, axis=0) > 0.5


def query_sum(own, nears, column):
    query = own(column, QUERY, QUERY + TOKENS)
    grad = own(column, GRAD, GRAD + TOKENS)
    stat = own(column, STAT, ROWS).astype(jnp.float32).T
    norm = stat[:, 0:1] + stat[:, 1:2] + stat[:, 2:3]
    delta = stat[:, 3:4] + stat[:, 4:5] + stat[:, 5:6]
    keys = near_all(nears, column, KEY)
    values = near_all(nears, column, VALUE)
    probs = jnp.exp2(dot_t(query, keys) * (SCALE * LOG2E) - norm)
    probs = jnp.where(tile_masks(column, 1, len(nears)), probs, 0.0)
    slope = probs * (dot_t(grad, values) - delta)
    return dot(slope.astype(jnp.bfloat16), keys)


def key_sum(owns, nears, column):
    key = jnp.concatenate([own(column, KEY, KEY + TOKENS) for own in owns], axis=0)
    value = jnp.concatenate([own(column, VALUE, VALUE + TOKENS) for own in owns], axis=0)
    queries = near_all(nears, column, QUERY)
    grads = near_all(nears, column, GRAD)
    norm = near_all_stat(nears, column, 0)
    delta = near_all_stat(nears, column, 3)
    probs = jnp.exp2(dot_t(key, queries) * (SCALE * LOG2E) - norm)
    probs = jnp.where(tile_masks(column, len(owns), len(nears)), probs, 0.0)
    value_sum = dot(probs.astype(jnp.bfloat16), grads)
    slope = probs * (dot_t(value, grads) - delta)
    return dot(slope.astype(jnp.bfloat16), queries), value_sum


def add_key_sums(totals, frames, column, parts):
    for i, frame in enumerate(frames):
        for total, part in zip(totals, parts):
            total[frame, column] += part[i * TOKENS : (i + 1) * TOKENS]


def by_core(ref, *index):
    return lambda block, lo, hi: ref[(block % 2, *index, block // 2, slice(lo, hi))]


def by_column(ref, *index):
    return lambda block, lo, hi: ref[(*index, block // 2, block % 2, slice(lo, hi))]


def frames_near(frame):
    return [f for f in range(FRAMES) if abs(f - frame) <= 1]


def edge_frame():
    return jnp.where(lax.axis_index("frame") < FRAMES, FRAMES - 1, 0)


def place(scratch, core, arrived, swapped):
    scratch[core] = arrived
    scratch[1 - core] = swapped


def first_query_kernel(arrived, swapped, total, blocks):
    core = lax.axis_index("space") % 2
    place(blocks, core, arrived[...], swapped[...])
    for frame in range(FRAMES):
        nears = [by_core(blocks, f, row) for f in frames_near(frame) for row in range(2)]
        for column in range(BLOCKS):
            total[frame, column] = query_sum(by_core(blocks, frame, core), nears, column)


def first_key_kernel(arrived, swapped, key_total, value_total, blocks):
    core = lax.axis_index("space") % 2
    place(blocks, core, arrived[...], swapped[...])
    key_total[...] = jnp.zeros_like(key_total)
    value_total[...] = jnp.zeros_like(value_total)
    for column in range(BLOCKS):
        for f in range(FRAMES):
            frames = frames_near(f)
            owns = [by_core(blocks, frame, core) for frame in frames]
            parts = key_sum(owns, [by_core(blocks, f, 0), by_core(blocks, f, 1)], column)
            add_key_sums((key_total, value_total), frames, column, parts)


def start_all(moves, sems):
    copies = [pltpu.make_async_copy(*move, sems.at[i]) for i, move in enumerate(moves)]
    for copy in copies:
        copy.start()
    return copies


def wait_all(copies):
    for copy in copies:
        copy.wait()


def finish(totals, firsts, column, done):
    for part, (total, first, scale) in enumerate(zip(totals, firsts, (SCALE, SCALE, 1.0))):
        rows = slice(part * TOKENS, (part + 1) * TOKENS)
        done[column % 2, ..., column // 2, rows, :] = ((total + first) * scale).astype(jnp.bfloat16)


def row_kernel(arrived, swapped, row, row_swapped, *rest):
    firsts, (mine, other, edges), rest = rest[:3], rest[3:6], rest[6:]
    own, near, done, first_totals, *totals, sems = rest
    core = lax.axis_index("space") % 2
    copies = start_all(
        [
            (arrived.at[:, core], own.at[core]),
            (swapped.at[:, core], own.at[1 - core]),
            (row.at[:, 1 - core], near.at[core]),
            (row_swapped, near.at[1 - core]),
        ]
        + [(first, first_totals.at[i]) for i, first in enumerate(firsts)],
        sems,
    )
    for total in totals[1:]:
        total[...] = jnp.zeros_like(total)
    wait_all(copies[:4])
    for column in range(BLOCKS):
        for f in range(FRAMES):
            frames = frames_near(f)
            owns = [by_core(own, frame) for frame in frames]
            parts = key_sum(owns, [by_core(near, f)], column)
            add_key_sums(totals[1:], frames, column, parts)
    for frame in range(FRAMES):
        nears = [by_core(near, f) for f in frames_near(frame)]
        for column in range(BLOCKS):
            totals[0][frame, column] = query_sum(by_core(own, frame), nears, column)
    wait_all(copies[4:])
    for column in range(BLOCKS):
        sums = [total[:, column] for total in totals]
        finish(sums, [first_totals[part, :, column] for part in range(3)], column, done)
    mine[...] = done[core]
    other[...] = done[1 - core]
    edge = edge_frame()
    for part, total in enumerate(totals):
        edges[part] = total[edge] + first_totals[part, edge]


def jump_kernel(arrived, swapped, jump, jump_swapped, jump_row, edges, mine_in, other_in, *rest):
    mine, other, own, jumped, jumped_row, sums, done, sems = rest
    core = lax.axis_index("space") % 2
    edge = edge_frame()
    copies = start_all(
        [
            (arrived.at[edge, core], own.at[core]),
            (swapped.at[edge, core], own.at[1 - core]),
            (jump, jumped.at[core]),
            (jump_swapped, jumped.at[1 - core]),
            (jump_row, jumped_row),
            (edges, sums),
        ],
        sems,
    )
    wait_all(copies)
    jumps = [by_core(jumped, 0), by_core(jumped, 1), by_column(jumped_row)]
    for column in range(BLOCKS):
        parts = (query_sum(by_core(own), jumps, column), *key_sum([by_core(own)], jumps, column))
        finish(parts, [sums[part, column] for part in range(3)], column, done)
    wait_all(start_all([(done.at[core], mine.at[edge]), (done.at[1 - core], other.at[edge])], sems))


KERNEL_FLOPS = 1 << 10
TOTALS = (FRAMES, BLOCKS, TOKENS, HEAD_DIM)
DONE = (FRAMES, 2, 3 * TOKENS, HEAD_DIM)


def attend(kernel, name, args, in_specs, out_specs, out_shape, scratch, aliases=None):
    return pl.pallas_call(
        kernel,
        out_shape=out_shape,
        in_specs=in_specs,
        out_specs=out_specs,
        scratch_shapes=scratch,
        input_output_aliases=aliases or {},
        compiler_params=params(),
        cost_estimate=pl.CostEstimate(
            flops=KERNEL_FLOPS, bytes_accessed=KERNEL_FLOPS, transcendentals=0
        ),
        name=name,
    )(*args)


def any_specs(count):
    return [pl.BlockSpec(memory_space=pl.ANY)] * count


def first_part(kernel, name, parts, *args):
    return attend(
        kernel,
        name,
        args,
        vmem_specs(len(args)),
        vmem_specs(parts),
        [jax.ShapeDtypeStruct(TOTALS, jnp.float32)] * parts,
        [pltpu.VMEM((2, FRAMES, 2, 2, ROWS, HEAD_DIM), jnp.bfloat16)],
    )


def row_part(*args):
    return attend(
        row_kernel,
        "row_part",
        args,
        any_specs(len(args)),
        vmem_specs(3),
        [jax.ShapeDtypeStruct(DONE, jnp.bfloat16)] * 2
        + [jax.ShapeDtypeStruct((3, *TOTALS[1:]), jnp.float32)],
        [
            pltpu.VMEM((2, FRAMES, 2, ROWS, HEAD_DIM), jnp.bfloat16),
            pltpu.VMEM((2, FRAMES, 2, ROWS, HEAD_DIM), jnp.bfloat16),
            pltpu.VMEM((2, *DONE), jnp.bfloat16),
            pltpu.VMEM((3, *TOTALS), jnp.float32),
        ]
        + [pltpu.VMEM(TOTALS, jnp.float32)] * 3
        + [pltpu.SemaphoreType.DMA((len(args),))],
    )


def jump_part(*args):
    return attend(
        jump_kernel,
        "jump_part",
        args,
        any_specs(len(args)),
        any_specs(2),
        [jax.ShapeDtypeStruct(DONE, jnp.bfloat16)] * 2,
        [
            pltpu.VMEM((2, 2, ROWS, HEAD_DIM), jnp.bfloat16),
            pltpu.VMEM((2, 2, 2, ROWS, HEAD_DIM), jnp.bfloat16),
            pltpu.VMEM((2, 2, ROWS, HEAD_DIM), jnp.bfloat16),
            pltpu.VMEM((3, *TOTALS[1:]), jnp.float32),
            pltpu.VMEM((2, *DONE[1:]), jnp.bfloat16),
            pltpu.SemaphoreType.DMA((len(args),)),
        ],
        {6: 0, 7: 1},
    )


def unpack_kernel(tile_valid, blocks, *outs):
    matrix = keep_matrix(tile_valid, 0)
    for part, out in enumerate(outs):
        rows = slice(part * TOKENS, (part + 1) * TOKENS)
        joined = jnp.concatenate([blocks[head, rows, :] for head in range(HEADS)], axis=1)
        out[...] = dot(matrix, joined).astype(jnp.bfloat16)


def unpack(tile_valid, blocks):
    shape = jax.ShapeDtypeStruct((TOKENS, HEADS * HEAD_DIM), jnp.bfloat16)
    return pl.pallas_call(
        unpack_kernel,
        out_shape=[shape] * 3,
        in_specs=[SMEM_SPEC] + vmem_specs(1),
        out_specs=vmem_specs(3),
        compiler_params=pltpu.CompilerParams(vmem_limit_bytes=VMEM_LIMIT // 3),
        name="unpack",
    )(tile_valid, blocks)


def plane_exchange(array):
    spaces = lax.axis_size("space")
    groups = []
    for half in range(lax.axis_size("frame") // FRAMES):
        for z in range(spaces // 8):
            for core in range(2):
                groups.append(
                    [
                        (half * FRAMES + j // 4) * spaces + z * 8 + (j % 4) * 2 + core
                        for j in range(CHIPS)
                    ]
                )
    return lax.all_to_all(array, AXES, 0, 0, axis_index_groups=groups)


def with_idle(array):
    return jnp.pad(array, ((0, CHIPS - HEADS), (0, 0), (0, 0)))


def core_swap(array):
    return lax.ppermute(array, "space", [(s, s ^ 1) for s in range(lax.axis_size("space"))])


def row_swap(array):
    route = []
    for s in range(1, lax.axis_size("space") - 8, 2):
        route += [(s, s + 7), (s + 7, s)]
    return lax.ppermute(array, "space", route)


def row_shift(array):
    count = lax.axis_size("space")
    route = [(s, s + (8 if s // 4 % 2 else -8)) for s in range(count)]
    return lax.ppermute(array, "space", [(a, b) for a, b in route if 0 <= b < count])


def half_swap(array):
    count = lax.axis_size("frame")
    return lax.ppermute(array, "frame", [(f, (f + FRAMES) % count) for f in range(count)])


def two_ways(core, mine, other, axis):
    first = jnp.where(core == 0, mine, other)
    second = jnp.where(core == 0, other, mine)
    return jnp.stack([first, second], axis=axis)


def own_row(core, arrived, swapped, axis):
    mine = lax.dynamic_index_in_dim(arrived, core, axis, keepdims=False)
    other = lax.dynamic_index_in_dim(swapped, core, axis, keepdims=False)
    return two_ways(core, mine, other, axis + 1)


def shards(query, key, value, grad_out, log_norm, delta, tile_valid):
    core = lax.axis_index("space") % 2
    shape = query.shape

    def flat(array):
        return array.reshape(TOKENS, array.shape[-1])

    heads, packed = pack(
        tile_valid, *(flat(v) for v in (key, value, query, grad_out, log_norm, delta))
    )
    shifted = refill(row_shift(heads))
    arrived = plane_exchange(packed)
    arrived, shifted = lax.optimization_barrier((arrived, shifted))
    arrived = arrived.reshape(FRAMES, 2, 2, ROWS, HEAD_DIM)
    jump = half_swap(lax.dynamic_index_in_dim(arrived, edge_frame(), 0, keepdims=False))
    swapped = core_swap(arrived)
    row = plane_exchange(shifted).reshape(FRAMES, 2, 2, ROWS, HEAD_DIM)
    firsts = [
        *first_part(first_query_kernel, "first_query", 1, arrived, swapped),
        *first_part(first_key_kernel, "first_key", 2, arrived, swapped),
    ]
    jump, firsts = lax.optimization_barrier((jump, firsts))
    jump_swapped = core_swap(jump)
    jump_row = row_swap(own_row(core, jump, jump_swapped, 0))
    row_swapped = core_swap(lax.dynamic_index_in_dim(row, core, 1, keepdims=False))
    mine, other, edges = row_part(arrived, swapped, row, row_swapped, *firsts)
    jump_row, edges = lax.optimization_barrier((jump_row, edges))
    mine, other = jump_part(
        arrived, swapped, jump, jump_swapped, jump_row, edges, mine, other
    )
    whole = two_ways(core, mine, core_swap(other), 1)
    blocks = plane_exchange(whole.reshape(CHIPS, *mine.shape[2:]))
    return tuple(out.reshape(shape) for out in unpack(tile_valid, blocks))


def solution(mesh):
    blocks = P("frame", "space", None, None, None)
    return jax.shard_map(
        shards,
        mesh=mesh,
        in_specs=(blocks,) * 6 + (P(),),
        out_specs=(blocks,) * 3,
        check_vma=False,
    )
```

```python
import functools
import math

import jax
import jax.numpy as jnp
from jax import lax
from jax.experimental import pallas as pl
from jax.experimental.pallas import tpu as pltpu
from jax.sharding import PartitionSpec as P

HEADS = 12
HEAD_DIM = 128
CHIPS = 16
BLOCKS = 4
FRAMES = 4
TOKENS = 128
HALF = 64
STAT_ROWS = 16
KEY, VALUE, QUERY, GRAD, STAT = (part * TOKENS for part in range(5))
ROWS = STAT + STAT_ROWS
RAW = GRAD
SCALE = 1.0 / math.sqrt(HEAD_DIM)
LOG2E = math.log2(math.e)
VMEM_LIMIT = 56 * 1024 * 1024
FILL_FLOPS = 1 << 34
AXES = ("frame", "space")

SMEM_SPEC = pl.BlockSpec(memory_space=pltpu.SMEM)


def vmem_specs(count):
    return [pl.BlockSpec(memory_space=pltpu.VMEM)] * count


def params():
    return pltpu.CompilerParams(vmem_limit_bytes=VMEM_LIMIT)


def keep_matrix(tile_valid, stored_dim):
    frame_valid = tile_valid[lax.axis_index("frame")]
    row_valid = tile_valid[lax.axis_size("frame") + lax.axis_index("space") // 4]
    tiled = lax.broadcasted_iota(jnp.int32, (TOKENS, TOKENS), 1 - stored_dim)
    stored = lax.broadcasted_iota(jnp.int32, (TOKENS, TOKENS), stored_dim)
    tile, frame = tiled >> 6, (tiled >> 4) & 3
    row, col = (tiled >> 2) & 3, tiled & 3
    same = stored == frame * 32 + row * 8 + tile * 4 + col
    keep = same & (frame < frame_valid) & (row < row_valid)
    return jnp.where(keep, 1.0, 0.0).astype(jnp.bfloat16)


def dot_t(a, b):
    return lax.dot_general(a, b, (((1,), (1,)), ((), ())), preferred_element_type=jnp.float32)


def dot(a, b):
    return jnp.dot(a, b, preferred_element_type=jnp.float32)


def pack_part(matrix, start, ref, out):
    moved = dot(matrix, ref[...]).astype(jnp.bfloat16)
    for head in range(HEADS):
        out[head, start : start + TOKENS, :] = moved[:, head * HEAD_DIM : (head + 1) * HEAD_DIM]


def pack_kernel(tile_valid, key, value, query, grad, log_norm, delta, out, raw, table):
    matrix = keep_matrix(tile_valid, 1)
    for start, ref in ((KEY, key), (VALUE, value), (QUERY, query), (GRAD, grad)):
        pack_part(matrix, start, ref, out)
    table[...] = jnp.zeros_like(table)
    for base, stat in ((0, log_norm[...] * LOG2E), (3, delta[...])):
        left = stat
        for step in range(3):
            piece = left.astype(jnp.bfloat16)
            left = left - piece.astype(jnp.float32)
            turned = dot(matrix, piece).T
            for head in range(HEADS):
                table[head, base + step : base + step + 1, :] = turned[head : head + 1, :]
    out[:HEADS, STAT:, :] = table[...].astype(jnp.bfloat16)
    out[HEADS:] = jnp.zeros((CHIPS - HEADS,) + out.shape[1:], jnp.bfloat16)
    raw[...] = out[:HEADS, :RAW, :]


PACKED_SHAPE = jax.ShapeDtypeStruct((CHIPS, ROWS, HEAD_DIM), jnp.bfloat16)
RAW_SHAPE = jax.ShapeDtypeStruct((HEADS, RAW, HEAD_DIM), jnp.bfloat16)
FILLED_SHAPE = jax.ShapeDtypeStruct((CHIPS, RAW, HEAD_DIM), jnp.bfloat16)


def pack(tile_valid, *arrays):
    return pl.pallas_call(
        pack_kernel,
        out_shape=[PACKED_SHAPE, RAW_SHAPE],
        in_specs=[SMEM_SPEC] + vmem_specs(len(arrays)),
        out_specs=vmem_specs(2),
        scratch_shapes=[pltpu.VMEM((HEADS, STAT_ROWS, TOKENS), jnp.float32)],
        compiler_params=params(),
        name="pack",
    )(tile_valid, *arrays)


def refill_kernel(heads, out, scratch, sems):
    pieces = [pl.ds(i * 3, 3) for i in range(HEADS // 3)]
    ins = [
        pltpu.make_async_copy(heads.at[piece], scratch.at[piece], sems.at[i])
        for i, piece in enumerate(pieces)
    ]
    for copy in ins:
        copy.start()
    scratch[HEADS:] = jnp.zeros((CHIPS - HEADS,) + out.shape[1:], jnp.bfloat16)
    pieces.append(pl.ds(HEADS, CHIPS - HEADS))
    outs = [
        pltpu.make_async_copy(scratch.at[piece], out.at[piece], sems.at[len(ins) + i])
        for i, piece in enumerate(pieces)
    ]
    outs[-1].start()
    for copy_in, copy_out in zip(ins, outs):
        copy_in.wait()
        copy_out.start()
    for copy in outs:
        copy.wait()


def refill(heads):
    return pl.pallas_call(
        refill_kernel,
        out_shape=FILLED_SHAPE,
        in_specs=[pl.BlockSpec(memory_space=pl.ANY)],
        out_specs=pl.BlockSpec(memory_space=pl.ANY),
        scratch_shapes=[
            pltpu.VMEM(FILLED_SHAPE.shape, jnp.bfloat16),
            pltpu.SemaphoreType.DMA((2 * (HEADS // 3) + 1,)),
        ],
        compiler_params=params(),
        cost_estimate=pl.CostEstimate(
            flops=FILL_FLOPS, bytes_accessed=FILL_FLOPS >> 8, transcendentals=0
        ),
        name="refill",
    )(heads)


def window(column):
    pieces = []
    if column > 0:
        pieces.append((column - 1, HALF, TOKENS))
    pieces.append((column, 0, TOKENS))
    if column < BLOCKS - 1:
        pieces.append((column + 1, 0, HALF))
    return pieces


def near_rows(near, column, offset):
    parts = [near(b, offset + lo, offset + hi) for b, lo, hi in window(column)]
    return jnp.concatenate(parts, axis=0)


def near_stat(near, column, base):
    parts = []
    for b, lo, hi in window(column):
        rows = near(b, STAT, ROWS).astype(jnp.float32)
        total = rows[base : base + 1] + rows[base + 1 : base + 2] + rows[base + 2 : base + 3]
        parts.append(total[:, lo:hi])
    return jnp.concatenate(parts, axis=1)


def tile_mask(column):
    extent = sum(hi - lo for _, lo, hi in window(column))
    skip = 1 if column > 0 else 0
    own = lax.broadcasted_iota(jnp.int32, (TOKENS, extent), 0) >> 6
    near = (lax.broadcasted_iota(jnp.int32, (TOKENS, extent), 1) >> 6) - skip
    return (own - near <= 1) & (near - own <= 1)


def reader(ref, *index):
    return lambda block, lo, hi: ref[(*index, block, slice(lo, hi), slice(None))]


def near_all(nears, column, offset):
    return jnp.concatenate([near_rows(near, column, offset) for near in nears], axis=0)


def near_all_stat(nears, column, base):
    return jnp.concatenate([near_stat(near, column, base) for near in nears], axis=1)


def tile_masks(column, own_count, near_count):
    one = jnp.where(tile_mask(column), 1.0, 0.0)
    line = jnp.concatenate([one] * near_count, axis=1)
    return jnp.concatenate([line] * own_count, axis=0) > 0.5


def query_sum(own, nears, column):
    query = own(column, QUERY, QUERY + TOKENS)
    grad = own(column, GRAD, GRAD + TOKENS)
    stat = own(column, STAT, ROWS).astype(jnp.float32).T
    norm = stat[:, 0:1] + stat[:, 1:2] + stat[:, 2:3]
    delta = stat[:, 3:4] + stat[:, 4:5] + stat[:, 5:6]
    keys = near_all(nears, column, KEY)
    values = near_all(nears, column, VALUE)
    probs = jnp.exp2(dot_t(query, keys) * (SCALE * LOG2E) - norm)
    probs = jnp.where(tile_masks(column, 1, len(nears)), probs, 0.0)
    slope = probs * (dot_t(grad, values) - delta)
    return dot(slope.astype(jnp.bfloat16), keys)


def key_sum(owns, nears, column):
    key = jnp.concatenate([own(column, KEY, KEY + TOKENS) for own in owns], axis=0)
    value = jnp.concatenate([own(column, VALUE, VALUE + TOKENS) for own in owns], axis=0)
    queries = near_all(nears, column, QUERY)
    grads = near_all(nears, column, GRAD)
    norm = near_all_stat(nears, column, 0)
    delta = near_all_stat(nears, column, 3)
    probs = jnp.exp2(dot_t(key, queries) * (SCALE * LOG2E) - norm)
    probs = jnp.where(tile_masks(column, len(owns), len(nears)), probs, 0.0)
    value_sum = dot(probs.astype(jnp.bfloat16), grads)
    slope = probs * (dot_t(value, grads) - delta)
    return dot(slope.astype(jnp.bfloat16), queries), value_sum


def add_key_sums(totals, frames, column, parts):
    for i, frame in enumerate(frames):
        for total, part in zip(totals, parts):
            total[frame, column] += part[i * TOKENS : (i + 1) * TOKENS]


def by_core(ref, *index):
    return lambda block, lo, hi: ref[(block % 2, *index, block // 2, slice(lo, hi))]


def by_either(raw, rest):
    return lambda block, lo, hi: raw(block, lo, hi) if hi <= RAW else rest(block, lo - RAW, hi - RAW)


def frames_near(frame):
    return [f for f in range(FRAMES) if abs(f - frame) <= 1]


def edge_frame():
    return jnp.where(lax.axis_index("frame") < FRAMES, FRAMES - 1, 0)


def place(scratch, core, arrived, swapped):
    scratch[core] = arrived
    scratch[1 - core] = swapped


def first_kernel(arrived, swapped, query_total, key_total, value_total, blocks):
    core = lax.axis_index("space") % 2
    place(blocks, core, arrived[...], swapped[...])
    for frame in range(FRAMES):
        nears = [by_core(blocks, f, row) for f in frames_near(frame) for row in range(2)]
        for column in range(BLOCKS):
            query_total[frame, column] = query_sum(by_core(blocks, frame, core), nears, column)
    key_total[...] = jnp.zeros_like(key_total)
    value_total[...] = jnp.zeros_like(value_total)
    for column in range(BLOCKS):
        for f in range(FRAMES):
            frames = frames_near(f)
            owns = [by_core(blocks, frame, core) for frame in frames]
            parts = key_sum(owns, [by_core(blocks, f, 0), by_core(blocks, f, 1)], column)
            add_key_sums((key_total, value_total), frames, column, parts)


def rest_kernel(arrived, swapped, out, sems):
    core = lax.axis_index("space") % 2
    rows = pl.ds(RAW, ROWS - RAW)
    wait_all(
        start_all(
            [
                (arrived.at[:, core, :, rows], out.at[core]),
                (swapped.at[:, core, :, rows], out.at[1 - core]),
            ],
            sems,
        )
    )


def start_all(moves, sems):
    copies = [pltpu.make_async_copy(*move, sems.at[i]) for i, move in enumerate(moves)]
    for copy in copies:
        copy.start()
    return copies


def wait_all(copies):
    for copy in copies:
        copy.wait()


def finish(totals, firsts, column, done):
    for part, (total, first, scale) in enumerate(zip(totals, firsts, (SCALE, SCALE, 1.0))):
        rows = slice(part * TOKENS, (part + 1) * TOKENS)
        done[column % 2, ..., column // 2, rows, :] = ((total + first) * scale).astype(jnp.bfloat16)


def row_kernel(arrived, swapped, row, row_swapped, row_rest, *rest):
    firsts, (mine, other, edges), rest = rest[:3], rest[3:6], rest[6:]
    own, near_raw, near_rest, done, first_totals, *totals, sems = rest
    core = lax.axis_index("space") % 2
    copies = start_all(
        [
            (arrived.at[:, core], own.at[core]),
            (swapped.at[:, core], own.at[1 - core]),
            (row.at[:, 1 - core], near_raw.at[core]),
            (row_swapped, near_raw.at[1 - core]),
            (row_rest, near_rest),
        ]
        + [(first, first_totals.at[i]) for i, first in enumerate(firsts)],
        sems,
    )

    def near(frame):
        return by_either(by_core(near_raw, frame), by_core(near_rest, frame))

    for total in totals[1:]:
        total[...] = jnp.zeros_like(total)
    wait_all(copies[:5])
    for column in range(BLOCKS):
        for f in range(FRAMES):
            frames = frames_near(f)
            owns = [by_core(own, frame) for frame in frames]
            parts = key_sum(owns, [near(f)], column)
            add_key_sums(totals[1:], frames, column, parts)
    for frame in range(FRAMES):
        nears = [near(f) for f in frames_near(frame)]
        for column in range(BLOCKS):
            totals[0][frame, column] = query_sum(by_core(own, frame), nears, column)
    wait_all(copies[5:])
    for column in range(BLOCKS):
        sums = [total[:, column] for total in totals]
        finish(sums, [first_totals[part, :, column] for part in range(3)], column, done)
    copies = start_all([(done.at[core], mine), (done.at[1 - core], other)], sems)
    edge = edge_frame()
    for part, total in enumerate(totals):
        edges[part] = total[edge] + first_totals[part, edge]
    wait_all(copies)


def jump_kernel(arrived, swapped, jump, jump_swapped, jump_row, edges, mine_in, other_in, *rest):
    mine, other, own, jumped, jumped_row, sums, done, sems = rest
    core = lax.axis_index("space") % 2
    edge = edge_frame()
    copies = start_all(
        [
            (arrived.at[edge, core], own.at[core]),
            (swapped.at[edge, core], own.at[1 - core]),
            (jump, jumped.at[core]),
            (jump_swapped, jumped.at[1 - core]),
            (jump_row, jumped_row),
            (edges, sums),
        ],
        sems,
    )
    wait_all(copies)
    jumps = [by_core(jumped, 0), by_core(jumped, 1), by_core(jumped_row)]
    for column in range(BLOCKS):
        parts = (query_sum(by_core(own), jumps, column), *key_sum([by_core(own)], jumps, column))
        finish(parts, [sums[part, column] for part in range(3)], column, done)
    wait_all(start_all([(done.at[core], mine.at[edge]), (done.at[1 - core], other.at[edge])], sems))


BORDER_FLOPS = 1 << 33
TOTALS = (FRAMES, BLOCKS, TOKENS, HEAD_DIM)
DONE = (FRAMES, 2, 3 * TOKENS, HEAD_DIM)


def attend(kernel, name, args, in_specs, out_specs, out_shape, scratch, aliases=None, flops=1 << 10, vmem=56):
    return pl.pallas_call(
        kernel,
        out_shape=out_shape,
        in_specs=in_specs,
        out_specs=out_specs,
        scratch_shapes=scratch,
        input_output_aliases=aliases or {},
        compiler_params=pltpu.CompilerParams(vmem_limit_bytes=vmem << 20),
        cost_estimate=pl.CostEstimate(
            flops=flops, bytes_accessed=flops >> 8, transcendentals=0
        ),
        name=name,
    )(*args)


def any_specs(count):
    return [pl.BlockSpec(memory_space=pl.ANY)] * count


def first_part(*args):
    return attend(
        first_kernel,
        "first_part",
        args,
        vmem_specs(len(args)),
        vmem_specs(3),
        [jax.ShapeDtypeStruct(TOTALS, jnp.float32)] * 3,
        [pltpu.VMEM((2, FRAMES, 2, 2, ROWS, HEAD_DIM), jnp.bfloat16)],
    )


def border_kernel(jump, jump_swapped, out):
    core = lax.axis_index("space") % 2
    place(out, core, jump[core], jump_swapped[core])


def border_part(*args):
    return attend(
        border_kernel,
        "border_part",
        args,
        vmem_specs(len(args)),
        vmem_specs(1),
        [jax.ShapeDtypeStruct((2, 2, ROWS, HEAD_DIM), jnp.bfloat16)],
        [],
        flops=BORDER_FLOPS,
        vmem=8,
    )[0]


def rest_part(*args):
    return attend(
        rest_kernel,
        "rest_part",
        args,
        any_specs(len(args)),
        vmem_specs(1),
        [jax.ShapeDtypeStruct((2, FRAMES, 2, ROWS - RAW, HEAD_DIM), jnp.bfloat16)],
        [pltpu.SemaphoreType.DMA((len(args),))],
    )[0]


def row_part(*args):
    return attend(
        row_kernel,
        "row_part",
        args,
        any_specs(len(args)),
        any_specs(2) + vmem_specs(1),
        [jax.ShapeDtypeStruct(DONE, jnp.bfloat16)] * 2
        + [jax.ShapeDtypeStruct((3, *TOTALS[1:]), jnp.float32)],
        [
            pltpu.VMEM((2, FRAMES, 2, ROWS, HEAD_DIM), jnp.bfloat16),
            pltpu.VMEM((2, FRAMES, 2, RAW, HEAD_DIM), jnp.bfloat16),
            pltpu.VMEM((2, FRAMES, 2, ROWS - RAW, HEAD_DIM), jnp.bfloat16),
            pltpu.VMEM((2, *DONE), jnp.bfloat16),
            pltpu.VMEM((3, *TOTALS), jnp.float32),
        ]
        + [pltpu.VMEM(TOTALS, jnp.float32)] * 3
        + [pltpu.SemaphoreType.DMA((len(args),))],
        vmem=32,
    )


def jump_part(*args):
    return attend(
        jump_kernel,
        "jump_part",
        args,
        any_specs(len(args)),
        any_specs(2),
        [jax.ShapeDtypeStruct(DONE, jnp.bfloat16)] * 2,
        [
            pltpu.VMEM((2, 2, ROWS, HEAD_DIM), jnp.bfloat16),
            pltpu.VMEM((2, 2, 2, ROWS, HEAD_DIM), jnp.bfloat16),
            pltpu.VMEM((2, 2, ROWS, HEAD_DIM), jnp.bfloat16),
            pltpu.VMEM((3, *TOTALS[1:]), jnp.float32),
            pltpu.VMEM((2, *DONE[1:]), jnp.bfloat16),
            pltpu.SemaphoreType.DMA((len(args),)),
        ],
        {6: 0, 7: 1},
        vmem=16,
    )


def unpack_kernel(tile_valid, blocks, *outs):
    matrix = keep_matrix(tile_valid, 0)
    for part, out in enumerate(outs):
        rows = slice(part * TOKENS, (part + 1) * TOKENS)
        joined = jnp.concatenate([blocks[head, rows, :] for head in range(HEADS)], axis=1)
        out[...] = dot(matrix, joined).astype(jnp.bfloat16)


def unpack(tile_valid, blocks):
    shape = jax.ShapeDtypeStruct((TOKENS, HEADS * HEAD_DIM), jnp.bfloat16)
    return pl.pallas_call(
        unpack_kernel,
        out_shape=[shape] * 3,
        in_specs=[SMEM_SPEC] + vmem_specs(1),
        out_specs=vmem_specs(3),
        compiler_params=pltpu.CompilerParams(vmem_limit_bytes=VMEM_LIMIT // 3),
        name="unpack",
    )(tile_valid, blocks)


def plane_exchange(array):
    spaces = lax.axis_size("space")
    groups = []
    for half in range(lax.axis_size("frame") // FRAMES):
        for z in range(spaces // 8):
            for core in range(2):
                groups.append(
                    [
                        (half * FRAMES + j // 4) * spaces + z * 8 + (j % 4) * 2 + core
                        for j in range(CHIPS)
                    ]
                )
    return lax.all_to_all(array, AXES, 0, 0, axis_index_groups=groups)


def with_idle(array):
    return jnp.pad(array, ((0, CHIPS - HEADS), (0, 0), (0, 0)))


def core_swap(array):
    return lax.ppermute(array, "space", [(s, s ^ 1) for s in range(lax.axis_size("space"))])


def row_swap(array):
    route = []
    for s in range(1, lax.axis_size("space") - 8, 2):
        route += [(s, s + 7), (s + 7, s)]
    return lax.ppermute(array, "space", route)


def row_shift(array):
    count = lax.axis_size("space")
    route = [(s, s + (8 if s // 4 % 2 else -8)) for s in range(count)]
    return lax.ppermute(array, "space", [(a, b) for a, b in route if 0 <= b < count])


def half_swap(array):
    count = lax.axis_size("frame")
    return lax.ppermute(array, "frame", [(f, (f + FRAMES) % count) for f in range(count)])


def two_ways(core, mine, other, axis):
    first = jnp.where(core == 0, mine, other)
    second = jnp.where(core == 0, other, mine)
    return jnp.stack([first, second], axis=axis)


def shards(query, key, value, grad_out, log_norm, delta, tile_valid):
    core = lax.axis_index("space") % 2
    shape = query.shape

    def flat(array):
        return array.reshape(TOKENS, array.shape[-1])

    packed, raw = pack(
        tile_valid, *(flat(v) for v in (key, value, query, grad_out, log_norm, delta))
    )
    shifted = refill(row_shift(raw))
    arrived = plane_exchange(packed)
    arrived, shifted = lax.optimization_barrier((arrived, shifted))
    arrived = arrived.reshape(FRAMES, 2, 2, ROWS, HEAD_DIM)
    jump = half_swap(lax.dynamic_index_in_dim(arrived, edge_frame(), 0, keepdims=False))
    swapped = core_swap(arrived)
    row = plane_exchange(shifted).reshape(FRAMES, 2, 2, RAW, HEAD_DIM)
    row_rest = row_swap(rest_part(arrived, swapped))
    firsts = first_part(arrived, swapped)
    jump, firsts = lax.optimization_barrier((jump, firsts))
    jump_swapped = core_swap(jump)
    jump_swapped, row_rest = lax.optimization_barrier((jump_swapped, row_rest))
    border = border_part(jump, jump_swapped)
    row, border = lax.optimization_barrier((row, border))
    jump_row = row_swap(border)
    row_swapped = core_swap(lax.dynamic_index_in_dim(row, core, 1, keepdims=False))
    mine, other, edges = row_part(arrived, swapped, row, row_swapped, row_rest, *firsts)
    jump_row, edges = lax.optimization_barrier((jump_row, edges))
    mine, other = jump_part(
        arrived, swapped, jump, jump_swapped, jump_row, edges, mine, other
    )
    whole = two_ways(core, mine, core_swap(other), 1)
    blocks = plane_exchange(whole.reshape(CHIPS, *mine.shape[2:]))
    return tuple(out.reshape(shape) for out in unpack(tile_valid, blocks))


def solution(mesh):
    blocks = P("frame", "space", None, None, None)
    return jax.shard_map(
        shards,
        mesh=mesh,
        in_specs=(blocks,) * 6 + (P(),),
        out_specs=(blocks,) * 3,
        check_vma=False,
    )
```

```python
import functools
import math

import jax
import jax.numpy as jnp
from jax import lax
from jax.experimental import pallas as pl
from jax.experimental.pallas import tpu as pltpu
from jax.sharding import PartitionSpec as P

HEADS = 12
HEAD_DIM = 128
CHIPS = 16
BLOCKS = 4
FRAMES = 4
TOKENS = 128
HALF = 64
STAT_ROWS = 16
KEY, VALUE, QUERY, GRAD, STAT = (part * TOKENS for part in range(5))
ROWS = STAT + STAT_ROWS
RAW = GRAD
SCALE = 1.0 / math.sqrt(HEAD_DIM)
LOG2E = math.log2(math.e)
VMEM_LIMIT = 56 * 1024 * 1024
FILL_FLOPS = 1 << 34
AXES = ("frame", "space")

SMEM_SPEC = pl.BlockSpec(memory_space=pltpu.SMEM)


def vmem_specs(count):
    return [pl.BlockSpec(memory_space=pltpu.VMEM)] * count


def params():
    return pltpu.CompilerParams(vmem_limit_bytes=VMEM_LIMIT)


def keep_matrix(tile_valid, stored_dim):
    frame_valid = tile_valid[lax.axis_index("frame")]
    row_valid = tile_valid[lax.axis_size("frame") + lax.axis_index("space") // 4]
    tiled = lax.broadcasted_iota(jnp.int32, (TOKENS, TOKENS), 1 - stored_dim)
    stored = lax.broadcasted_iota(jnp.int32, (TOKENS, TOKENS), stored_dim)
    tile, frame = tiled >> 6, (tiled >> 4) & 3
    row, col = (tiled >> 2) & 3, tiled & 3
    same = stored == frame * 32 + row * 8 + tile * 4 + col
    keep = same & (frame < frame_valid) & (row < row_valid)
    return jnp.where(keep, 1.0, 0.0).astype(jnp.bfloat16)


def dot_t(a, b):
    return lax.dot_general(a, b, (((1,), (1,)), ((), ())), preferred_element_type=jnp.float32)


def dot(a, b):
    return jnp.dot(a, b, preferred_element_type=jnp.float32)


def pack_part(matrix, start, ref, out):
    moved = dot(matrix, ref[...]).astype(jnp.bfloat16)
    for head in range(HEADS):
        out[head, start : start + TOKENS, :] = moved[:, head * HEAD_DIM : (head + 1) * HEAD_DIM]


def pack_kernel(tile_valid, key, value, query, grad, log_norm, delta, out, raw, table):
    matrix = keep_matrix(tile_valid, 1)
    for start, ref in ((KEY, key), (VALUE, value), (QUERY, query), (GRAD, grad)):
        pack_part(matrix, start, ref, out)
    table[...] = jnp.zeros_like(table)
    for base, stat in ((0, log_norm[...] * LOG2E), (3, delta[...])):
        left = stat
        for step in range(3):
            piece = left.astype(jnp.bfloat16)
            left = left - piece.astype(jnp.float32)
            turned = dot(matrix, piece).T
            for head in range(HEADS):
                table[head, base + step : base + step + 1, :] = turned[head : head + 1, :]
    out[:HEADS, STAT:, :] = table[...].astype(jnp.bfloat16)
    out[HEADS:] = jnp.zeros((CHIPS - HEADS,) + out.shape[1:], jnp.bfloat16)
    raw[...] = out[:HEADS, :RAW, :]


PACKED_SHAPE = jax.ShapeDtypeStruct((CHIPS, ROWS, HEAD_DIM), jnp.bfloat16)
RAW_SHAPE = jax.ShapeDtypeStruct((HEADS, RAW, HEAD_DIM), jnp.bfloat16)
FILLED_SHAPE = jax.ShapeDtypeStruct((CHIPS, RAW, HEAD_DIM), jnp.bfloat16)


def pack(tile_valid, *arrays):
    return pl.pallas_call(
        pack_kernel,
        out_shape=[PACKED_SHAPE, RAW_SHAPE],
        in_specs=[SMEM_SPEC] + vmem_specs(len(arrays)),
        out_specs=vmem_specs(2),
        scratch_shapes=[pltpu.VMEM((HEADS, STAT_ROWS, TOKENS), jnp.float32)],
        compiler_params=params(),
        name="pack",
    )(tile_valid, *arrays)


def refill_kernel(heads, out, scratch, sems):
    pieces = [pl.ds(i * 3, 3) for i in range(HEADS // 3)]
    ins = [
        pltpu.make_async_copy(heads.at[piece], scratch.at[piece], sems.at[i])
        for i, piece in enumerate(pieces)
    ]
    for copy in ins:
        copy.start()
    scratch[HEADS:] = jnp.zeros((CHIPS - HEADS,) + out.shape[1:], jnp.bfloat16)
    pieces.append(pl.ds(HEADS, CHIPS - HEADS))
    outs = [
        pltpu.make_async_copy(scratch.at[piece], out.at[piece], sems.at[len(ins) + i])
        for i, piece in enumerate(pieces)
    ]
    outs[-1].start()
    for copy_in, copy_out in zip(ins, outs):
        copy_in.wait()
        copy_out.start()
    for copy in outs:
        copy.wait()


def refill(heads):
    return pl.pallas_call(
        refill_kernel,
        out_shape=FILLED_SHAPE,
        in_specs=[pl.BlockSpec(memory_space=pl.ANY)],
        out_specs=pl.BlockSpec(memory_space=pl.ANY),
        scratch_shapes=[
            pltpu.VMEM(FILLED_SHAPE.shape, jnp.bfloat16),
            pltpu.SemaphoreType.DMA((2 * (HEADS // 3) + 1,)),
        ],
        compiler_params=params(),
        cost_estimate=pl.CostEstimate(
            flops=FILL_FLOPS, bytes_accessed=FILL_FLOPS >> 8, transcendentals=0
        ),
        name="refill",
    )(heads)


def window(column):
    pieces = []
    if column > 0:
        pieces.append((column - 1, HALF, TOKENS))
    pieces.append((column, 0, TOKENS))
    if column < BLOCKS - 1:
        pieces.append((column + 1, 0, HALF))
    return pieces


def near_rows(near, column, offset):
    parts = [near(b, offset + lo, offset + hi) for b, lo, hi in window(column)]
    return jnp.concatenate(parts, axis=0)


def near_stat(near, column, base):
    parts = []
    for b, lo, hi in window(column):
        rows = near(b, STAT, ROWS).astype(jnp.float32)
        total = rows[base : base + 1] + rows[base + 1 : base + 2] + rows[base + 2 : base + 3]
        parts.append(total[:, lo:hi])
    return jnp.concatenate(parts, axis=1)


def tile_mask(column):
    extent = sum(hi - lo for _, lo, hi in window(column))
    skip = 1 if column > 0 else 0
    own = lax.broadcasted_iota(jnp.int32, (TOKENS, extent), 0) >> 6
    near = (lax.broadcasted_iota(jnp.int32, (TOKENS, extent), 1) >> 6) - skip
    return (own - near <= 1) & (near - own <= 1)


def reader(ref, *index):
    return lambda block, lo, hi: ref[(*index, block, slice(lo, hi), slice(None))]


def near_all(nears, column, offset):
    return jnp.concatenate([near_rows(near, column, offset) for near in nears], axis=0)


def near_all_stat(nears, column, base):
    return jnp.concatenate([near_stat(near, column, base) for near in nears], axis=1)


def tile_masks(column, own_count, near_count):
    one = jnp.where(tile_mask(column), 1.0, 0.0)
    line = jnp.concatenate([one] * near_count, axis=1)
    return jnp.concatenate([line] * own_count, axis=0) > 0.5


def query_sum(own, nears, column):
    query = own(column, QUERY, QUERY + TOKENS)
    grad = own(column, GRAD, GRAD + TOKENS)
    stat = own(column, STAT, ROWS).astype(jnp.float32).T
    norm = stat[:, 0:1] + stat[:, 1:2] + stat[:, 2:3]
    delta = stat[:, 3:4] + stat[:, 4:5] + stat[:, 5:6]
    keys = near_all(nears, column, KEY)
    values = near_all(nears, column, VALUE)
    probs = jnp.exp2(dot_t(query, keys) * (SCALE * LOG2E) - norm)
    probs = jnp.where(tile_masks(column, 1, len(nears)), probs, 0.0)
    slope = probs * (dot_t(grad, values) - delta)
    return dot(slope.astype(jnp.bfloat16), keys)


def key_sum(owns, nears, column):
    key = jnp.concatenate([own(column, KEY, KEY + TOKENS) for own in owns], axis=0)
    value = jnp.concatenate([own(column, VALUE, VALUE + TOKENS) for own in owns], axis=0)
    queries = near_all(nears, column, QUERY)
    grads = near_all(nears, column, GRAD)
    norm = near_all_stat(nears, column, 0)
    delta = near_all_stat(nears, column, 3)
    probs = jnp.exp2(dot_t(key, queries) * (SCALE * LOG2E) - norm)
    probs = jnp.where(tile_masks(column, len(owns), len(nears)), probs, 0.0)
    value_sum = dot(probs.astype(jnp.bfloat16), grads)
    slope = probs * (dot_t(value, grads) - delta)
    return dot(slope.astype(jnp.bfloat16), queries), value_sum


def add_key_sums(totals, frames, column, parts):
    for i, frame in enumerate(frames):
        for total, part in zip(totals, parts):
            total[frame, column] += part[i * TOKENS : (i + 1) * TOKENS]


def by_core(ref, *index):
    return lambda block, lo, hi: ref[(block % 2, *index, block // 2, slice(lo, hi))]


def by_either(raw, rest):
    return lambda block, lo, hi: raw(block, lo, hi) if hi <= RAW else rest(block, lo - RAW, hi - RAW)


def frames_near(frame):
    return [f for f in range(FRAMES) if abs(f - frame) <= 1]


def edge_frame():
    return jnp.where(lax.axis_index("frame") < FRAMES, FRAMES - 1, 0)


def place(scratch, core, arrived, swapped):
    scratch[core] = arrived
    scratch[1 - core] = swapped


def first_kernel(arrived, swapped, query_total, key_total, value_total, blocks):
    core = lax.axis_index("space") % 2
    place(blocks, core, arrived[...], swapped[...])
    for frame in range(FRAMES):
        nears = [by_core(blocks, f, row) for f in frames_near(frame) for row in range(2)]
        for column in range(BLOCKS):
            query_total[frame, column] = query_sum(by_core(blocks, frame, core), nears, column)
    key_total[...] = jnp.zeros_like(key_total)
    value_total[...] = jnp.zeros_like(value_total)
    for column in range(BLOCKS):
        for f in range(FRAMES):
            frames = frames_near(f)
            owns = [by_core(blocks, frame, core) for frame in frames]
            parts = key_sum(owns, [by_core(blocks, f, 0), by_core(blocks, f, 1)], column)
            add_key_sums((key_total, value_total), frames, column, parts)


def rest_kernel(arrived, swapped, out, sems):
    core = lax.axis_index("space") % 2
    rows = pl.ds(RAW, ROWS - RAW)
    wait_all(
        start_all(
            [
                (arrived.at[:, core, :, rows], out.at[core]),
                (swapped.at[:, core, :, rows], out.at[1 - core]),
            ],
            sems,
        )
    )


def start_all(moves, sems):
    copies = [pltpu.make_async_copy(*move, sems.at[i]) for i, move in enumerate(moves)]
    for copy in copies:
        copy.start()
    return copies


def wait_all(copies):
    for copy in copies:
        copy.wait()


def finish(totals, firsts, column, done):
    for part, (total, first, scale) in enumerate(zip(totals, firsts, (SCALE, SCALE, 1.0))):
        rows = slice(part * TOKENS, (part + 1) * TOKENS)
        done[column % 2, ..., column // 2, rows, :] = ((total + first) * scale).astype(jnp.bfloat16)


def row_kernel(_, arrived, swapped, row, row_swapped, row_rest, *rest):
    firsts, (mine, other, edges), rest = rest[:3], rest[3:6], rest[6:]
    own, near_raw, near_rest, done, first_totals, *totals, sems = rest
    core = lax.axis_index("space") % 2
    copies = start_all(
        [
            (arrived.at[:, core], own.at[core]),
            (swapped.at[:, core], own.at[1 - core]),
            (row.at[:, 1 - core], near_raw.at[core]),
            (row_swapped, near_raw.at[1 - core]),
            (row_rest, near_rest),
        ]
        + [(first, first_totals.at[i]) for i, first in enumerate(firsts)],
        sems,
    )

    def near(frame):
        return by_either(by_core(near_raw, frame), by_core(near_rest, frame))

    for total in totals[1:]:
        total[...] = jnp.zeros_like(total)
    wait_all(copies[:5])
    for column in range(BLOCKS):
        for f in range(FRAMES):
            frames = frames_near(f)
            owns = [by_core(own, frame) for frame in frames]
            parts = key_sum(owns, [near(f)], column)
            add_key_sums(totals[1:], frames, column, parts)
    for frame in range(FRAMES):
        nears = [near(f) for f in frames_near(frame)]
        for column in range(BLOCKS):
            totals[0][frame, column] = query_sum(by_core(own, frame), nears, column)
    wait_all(copies[5:])
    for column in range(BLOCKS):
        sums = [total[:, column] for total in totals]
        finish(sums, [first_totals[part, :, column] for part in range(3)], column, done)
    copies = start_all([(done.at[core], mine), (done.at[1 - core], other)], sems)
    edge = edge_frame()
    for part, total in enumerate(totals):
        edges[part] = total[edge] + first_totals[part, edge]
    wait_all(copies)


def jump_kernel(arrived, swapped, jump, jump_swapped, jump_row, edges, mine_in, other_in, *rest):
    mine, other, own, jumped, jumped_row, sums, done, sems = rest
    core = lax.axis_index("space") % 2
    edge = edge_frame()
    copies = start_all(
        [
            (arrived.at[edge, core], own.at[core]),
            (swapped.at[edge, core], own.at[1 - core]),
            (jump, jumped.at[core]),
            (jump_swapped, jumped.at[1 - core]),
            (jump_row, jumped_row),
            (edges, sums),
        ],
        sems,
    )
    wait_all(copies)
    jumps = [by_core(jumped, 0), by_core(jumped, 1), by_core(jumped_row)]
    for column in range(BLOCKS):
        parts = (query_sum(by_core(own), jumps, column), *key_sum([by_core(own)], jumps, column))
        finish(parts, [sums[part, column] for part in range(3)], column, done)
    wait_all(start_all([(done.at[core], mine.at[edge]), (done.at[1 - core], other.at[edge])], sems))


GATE_FLOPS = 1 << 33
TOTALS = (FRAMES, BLOCKS, TOKENS, HEAD_DIM)
DONE = (FRAMES, 2, 3 * TOKENS, HEAD_DIM)


def attend(kernel, name, args, in_specs, out_specs, out_shape, scratch, aliases=None, flops=1 << 10, vmem=56):
    return pl.pallas_call(
        kernel,
        out_shape=out_shape,
        in_specs=in_specs,
        out_specs=out_specs,
        scratch_shapes=scratch,
        input_output_aliases=aliases or {},
        compiler_params=pltpu.CompilerParams(vmem_limit_bytes=vmem << 20),
        cost_estimate=pl.CostEstimate(
            flops=flops, bytes_accessed=flops >> 8, transcendentals=0
        ),
        name=name,
    )(*args)


def any_specs(count):
    return [pl.BlockSpec(memory_space=pl.ANY)] * count


def first_part(*args):
    return attend(
        first_kernel,
        "first_part",
        args,
        vmem_specs(len(args)),
        vmem_specs(3),
        [jax.ShapeDtypeStruct(TOTALS, jnp.float32)] * 3,
        [pltpu.VMEM((2, FRAMES, 2, 2, ROWS, HEAD_DIM), jnp.bfloat16)],
        vmem=56,
    )


def border_kernel(jump, jump_swapped, out):
    core = lax.axis_index("space") % 2
    place(out, core, jump[core], jump_swapped[core])


def border_part(*args):
    return attend(
        border_kernel,
        "border_part",
        args,
        vmem_specs(len(args)),
        vmem_specs(1),
        [jax.ShapeDtypeStruct((2, 2, ROWS, HEAD_DIM), jnp.bfloat16)],
        [],
        vmem=8,
    )[0]


def gate_kernel(border, out):
    out[...] = border[...]


def gate_part(border):
    shape = (1, 1, STAT_ROWS, HEAD_DIM)
    block = pl.BlockSpec(shape, lambda i: (0, 0, 0, 0))
    return pl.pallas_call(
        gate_kernel,
        grid=(1,),
        out_shape=jax.ShapeDtypeStruct(shape, jnp.bfloat16),
        in_specs=[block],
        out_specs=block,
        compiler_params=pltpu.CompilerParams(vmem_limit_bytes=8 << 20),
        cost_estimate=pl.CostEstimate(
            flops=GATE_FLOPS, bytes_accessed=GATE_FLOPS >> 8, transcendentals=0
        ),
        name="gate",
    )(border)


def rest_part(*args):
    return attend(
        rest_kernel,
        "rest_part",
        args,
        any_specs(len(args)),
        vmem_specs(1),
        [jax.ShapeDtypeStruct((2, FRAMES, 2, ROWS - RAW, HEAD_DIM), jnp.bfloat16)],
        [pltpu.SemaphoreType.DMA((len(args),))],
    )[0]


def row_part(*args):
    return attend(
        row_kernel,
        "row_part",
        args,
        any_specs(len(args)),
        any_specs(2) + vmem_specs(1),
        [jax.ShapeDtypeStruct(DONE, jnp.bfloat16)] * 2
        + [jax.ShapeDtypeStruct((3, *TOTALS[1:]), jnp.float32)],
        [
            pltpu.VMEM((2, FRAMES, 2, ROWS, HEAD_DIM), jnp.bfloat16),
            pltpu.VMEM((2, FRAMES, 2, RAW, HEAD_DIM), jnp.bfloat16),
            pltpu.VMEM((2, FRAMES, 2, ROWS - RAW, HEAD_DIM), jnp.bfloat16),
            pltpu.VMEM((2, *DONE), jnp.bfloat16),
            pltpu.VMEM((3, *TOTALS), jnp.float32),
        ]
        + [pltpu.VMEM(TOTALS, jnp.float32)] * 3
        + [pltpu.SemaphoreType.DMA((len(args),))],
        vmem=46,
    )


def jump_part(*args):
    return attend(
        jump_kernel,
        "jump_part",
        args,
        any_specs(len(args)),
        any_specs(2),
        [jax.ShapeDtypeStruct(DONE, jnp.bfloat16)] * 2,
        [
            pltpu.VMEM((2, 2, ROWS, HEAD_DIM), jnp.bfloat16),
            pltpu.VMEM((2, 2, 2, ROWS, HEAD_DIM), jnp.bfloat16),
            pltpu.VMEM((2, 2, ROWS, HEAD_DIM), jnp.bfloat16),
            pltpu.VMEM((3, *TOTALS[1:]), jnp.float32),
            pltpu.VMEM((2, *DONE[1:]), jnp.bfloat16),
            pltpu.SemaphoreType.DMA((len(args),)),
        ],
        {6: 0, 7: 1},
        vmem=16,
    )


def unpack_kernel(tile_valid, blocks, *outs):
    matrix = keep_matrix(tile_valid, 0)
    for part, out in enumerate(outs):
        rows = slice(part * TOKENS, (part + 1) * TOKENS)
        joined = jnp.concatenate([blocks[head, rows, :] for head in range(HEADS)], axis=1)
        out[...] = dot(matrix, joined).astype(jnp.bfloat16)


def unpack(tile_valid, blocks):
    shape = jax.ShapeDtypeStruct((TOKENS, HEADS * HEAD_DIM), jnp.bfloat16)
    return pl.pallas_call(
        unpack_kernel,
        out_shape=[shape] * 3,
        in_specs=[SMEM_SPEC] + vmem_specs(1),
        out_specs=vmem_specs(3),
        compiler_params=pltpu.CompilerParams(vmem_limit_bytes=VMEM_LIMIT // 3),
        name="unpack",
    )(tile_valid, blocks)


def plane_exchange(array):
    spaces = lax.axis_size("space")
    groups = []
    for half in range(lax.axis_size("frame") // FRAMES):
        for z in range(spaces // 8):
            for core in range(2):
                groups.append(
                    [
                        (half * FRAMES + j // 4) * spaces + z * 8 + (j % 4) * 2 + core
                        for j in range(CHIPS)
                    ]
                )
    return lax.all_to_all(array, AXES, 0, 0, axis_index_groups=groups)


def with_idle(array):
    return jnp.pad(array, ((0, CHIPS - HEADS), (0, 0), (0, 0)))


def core_swap(array):
    return lax.ppermute(array, "space", [(s, s ^ 1) for s in range(lax.axis_size("space"))])


def row_swap(array):
    route = []
    for s in range(1, lax.axis_size("space") - 8, 2):
        route += [(s, s + 7), (s + 7, s)]
    return lax.ppermute(array, "space", route)


def row_shift(array):
    count = lax.axis_size("space")
    route = [(s, s + (8 if s // 4 % 2 else -8)) for s in range(count)]
    return lax.ppermute(array, "space", [(a, b) for a, b in route if 0 <= b < count])


def half_swap(array):
    count = lax.axis_size("frame")
    return lax.ppermute(array, "frame", [(f, (f + FRAMES) % count) for f in range(count)])


def two_ways(core, mine, other, axis):
    first = jnp.where(core == 0, mine, other)
    second = jnp.where(core == 0, other, mine)
    return jnp.stack([first, second], axis=axis)


def shards(query, key, value, grad_out, log_norm, delta, tile_valid):
    core = lax.axis_index("space") % 2
    shape = query.shape

    def flat(array):
        return array.reshape(TOKENS, array.shape[-1])

    packed, raw = pack(
        tile_valid, *(flat(v) for v in (key, value, query, grad_out, log_norm, delta))
    )
    shifted = refill(row_shift(raw))
    arrived = plane_exchange(packed)
    arrived, shifted = lax.optimization_barrier((arrived, shifted))
    arrived = arrived.reshape(FRAMES, 2, 2, ROWS, HEAD_DIM)
    jump = half_swap(lax.dynamic_index_in_dim(arrived, edge_frame(), 0, keepdims=False))
    swapped = core_swap(arrived)
    row = plane_exchange(shifted).reshape(FRAMES, 2, 2, RAW, HEAD_DIM)
    row_rest = row_swap(rest_part(arrived, swapped))
    firsts = first_part(arrived, swapped)
    jump, firsts = lax.optimization_barrier((jump, firsts))
    jump_swapped = core_swap(jump)
    border = border_part(jump, jump_swapped)
    jump_row = row_swap(border)
    gated, row_rest = lax.optimization_barrier((border, row_rest))
    row, gate = lax.optimization_barrier((row, gate_part(gated)))
    row_swapped = core_swap(lax.dynamic_index_in_dim(row, core, 1, keepdims=False))
    mine, other, edges = row_part(gate, arrived, swapped, row, row_swapped, row_rest, *firsts)
    jump_row, edges = lax.optimization_barrier((jump_row, edges))
    mine, other = jump_part(
        arrived, swapped, jump, jump_swapped, jump_row, edges, mine, other
    )
    whole = two_ways(core, mine, core_swap(other), 1)
    blocks = plane_exchange(whole.reshape(CHIPS, *mine.shape[2:]))
    return tuple(out.reshape(shape) for out in unpack(tile_valid, blocks))


def solution(mesh):
    blocks = P("frame", "space", None, None, None)
    return jax.shard_map(
        shards,
        mesh=mesh,
        in_specs=(blocks,) * 6 + (P(),),
        out_specs=(blocks,) * 3,
        check_vma=False,
    )
```
